512 devices in a mesh: slab: 128 (over x, z, y_lo), row: 4 (over y_hi, core).
Axes of the slice: x: 4, y: 4 (y_hi: 2, y_lo: 2; y = y_hi * 2 + y_lo), z: 16, core: 2. Of those that a mesh axis runs over, the one named last changes fastest.
Arguments:
- image: bfloat16 [512, 128, 128], P('slab', 'row'), may hold values from -6 to 6
- first_kernel: bfloat16 [3, 3, 32, 1], replicated, may hold values from -2 to 2
- first_bias: float32 [32], replicated, may hold values from -1.5 to 1.5
- middle_kernel: bfloat16 [3, 3, 32, 32], replicated, may hold values from -0.5 to 0.5
- middle_bias: float32 [32], replicated, may hold values from -1.5 to 1.5
- last_kernel: bfloat16 [3, 3, 3, 32], replicated, may hold values from -0.5 to 0.5
- last_bias: float32 [3], replicated, may hold values from -2 to 2
Outputs:
- flows: float32 [4, 512, 128, 128], P(None, 'slab', 'row')
The draws below stay inside these ranges and needn't reach their ends.
All inputs are finite; a program needn't handle non-finite values.
Results may differ from the reference program's by a relative error of at most 0.0052.
Values may be sent and summed in bfloat16 or wider, within the bound.
A program may use at most 64 MiB of HBM per device.

```python
import jax
import jax.numpy as jnp
from jax import lax

CH = 32
Z = 512
Y = 128
X = 128


def levels(stream_key, dims, shards, least, largest):
    level = 1.0
    for position, parts in shards:
        heights = jax.random.uniform(jax.random.fold_in(jax.random.fold_in(stream_key, 6), position), (parts,), jnp.float32, least / len(shards), largest / len(shards))
        level = level * jnp.repeat(jnp.exp(heights), dims[position] // parts).reshape((-1,) + (1,) * (len(dims) - 1 - position))
    return level


def noise(stream_key, shape, spread, reach, pieces=(), kind=jnp.bfloat16):
    drawn = spread * jax.random.normal(stream_key, shape, jnp.float32)
    if pieces:
        drawn = drawn * levels(stream_key, shape, pieces, -0.22, 0.18)
    return jnp.clip(drawn, -reach, reach).astype(kind)


def setup_inputs(seed: int = 0) -> dict:
    key_of = jax.random.split(jax.random.key(seed), 8)
    return {
        "image": noise(key_of[0], (Z, Y, X), 1.0, 6.0, ((0, 128), (1, 4))),
        "first_kernel": noise(key_of[1], (3, 3, CH, 1), 9 ** -0.5, 2.0),
        "first_bias": noise(key_of[2], (CH,), 0.3, 1.5, (), jnp.float32),
        "middle_kernel": noise(key_of[3], (3, 3, CH, CH), (9 * CH // 2) ** -0.5, 0.5),
        "middle_bias": noise(key_of[4], (CH,), 0.3, 1.5, (), jnp.float32),
        "last_kernel": noise(key_of[5], (3, 3, 3, CH), (9 * CH // 2) ** -0.5, 0.5),
        "last_bias": noise(key_of[6], (3,), 0.5, 2.0, (), jnp.float32),
    }


def convolve(values, kernel):
    return lax.conv_general_dilated(values, kernel.astype(jnp.float32), (1, 1), ((1, 1), (1, 1)),
                                    dimension_numbers=("NCHW", "HWOI", "NCHW"),
                                    precision=lax.Precision.HIGHEST)


def network(planes, params):
    first_kernel, first_bias, middle_kernel, middle_bias, last_kernel, last_bias = params
    hidden_one = jax.nn.relu(convolve(planes[:, None].astype(jnp.float32), first_kernel)
                             + first_bias[None, :, None, None]).astype(jnp.bfloat16)
    hidden_two = jax.nn.relu(convolve(hidden_one.astype(jnp.float32), middle_kernel)
                             + middle_bias[None, :, None, None]).astype(jnp.bfloat16)
    return convolve(hidden_two.astype(jnp.float32), last_kernel) + last_bias[None, :, None, None]


def reference(image, first_kernel, first_bias, middle_kernel, middle_bias, last_kernel, last_bias):
    params = (first_kernel, first_bias, middle_kernel, middle_bias, last_kernel, last_bias)

    def single(plane):
        return network(plane[None], params)[0]

    xy_flows = lax.map(single, image, batch_size=8)
    yz_flows = lax.map(single, image.transpose(2, 0, 1), batch_size=8)
    yz_zero = yz_flows[:, 0].transpose(1, 2, 0)
    yz_one = yz_flows[:, 1].transpose(1, 2, 0)
    yz_two = yz_flows[:, 2].transpose(1, 2, 0)
    return jnp.stack([yz_zero, 0.5 * (xy_flows[:, 0] + yz_one), xy_flows[:, 1],
                      0.5 * (xy_flows[:, 2] + yz_two)])
```

```python
import jax
import jax.numpy as jnp
from jax import lax
from jax.experimental import pallas as pl
from jax.experimental.pallas import tpu as pltpu
from jax.sharding import PartitionSpec as P

MESH = pl.DeviceIdType.MESH
F32 = jnp.float32
BF16 = jnp.bfloat16

SIDES = [(ds, dr) for ds in (-1, 0, 1) for dr in (-1, 0, 1) if ds or dr]
RUN = 32


def iota(shape, dim):
    return lax.broadcasted_iota(jnp.int32, shape, dim)


def spread(rows, lanes):
    return ((iota((rows, lanes), 1) & 31) == iota((rows, lanes), 0)).astype(BF16)


def dot(a, b):
    return jnp.dot(a, b, preferred_element_type=F32)


def span(step, own, low, high):
    return {0: own, 1: low, -1: high}[step]


def exchange_kernel(
    img, k1, b1, k2, b2, k3, b3,
    ext, w1z, w2z, w3z, b2c, brow, xyp,
    k1v, b1v, k2v, b2v, k3v, b3v, w1x, w2x, w3x, imx, h1c, h1l, h1r, h2x,
    load_sem, send_sem, recv_sem,
):
    s = lax.axis_index("slab")
    r = lax.axis_index("row")
    slabs = lax.axis_size("slab")
    rows = lax.axis_size("row")
    place = lax.rem(s, RUN)

    def inside(ds, dr):
        return (s + ds >= 0) & (s + ds < slabs) & (r + dr >= 0) & (r + dr < rows)

    def later(ds, dr):
        if ds == 0:
            return jnp.bool_(dr > 0)
        if ds > 0:
            return place != RUN - 1
        return place == 0

    barrier = pltpu.get_barrier_semaphore()
    greeted = jnp.int32(0)
    for ds, dr in SIDES:
        here = inside(ds, dr)
        after = later(ds, dr)
        greeted += (here & ~after).astype(jnp.int32)

        @pl.when(here & after)
        def _():
            pl.semaphore_signal(barrier, inc=1, device_id=(s + ds, r + dr), device_id_type=MESH)

    copies = []
    for n, (ds, dr) in enumerate(SIDES):
        zs, zd = span(ds, ((0, 4), (3, 7)), ((1, 4), (0, 3)), ((0, 3), (7, 10)))
        ys, yd = span(dr, ((0, 32), (16, 48)), ((16, 32), (0, 16)), ((0, 16), (48, 64)))
        copies.append(
            pltpu.make_async_remote_copy(
                src_ref=img.at[zs[0] : zs[1], ys[0] : ys[1]],
                dst_ref=ext.at[zd[0] : zd[1], yd[0] : yd[1]],
                send_sem=send_sem.at[n],
                recv_sem=recv_sem.at[n],
                device_id=(s + ds, r + dr),
                device_id_type=MESH,
            )
        )

    @pl.when(greeted > 0)
    def _():
        pl.semaphore_wait(barrier, greeted)

    for n, (ds, dr) in enumerate(SIDES):

        @pl.when(inside(ds, dr) & ~later(ds, dr))
        def _():
            copies[n].start()

    loads = [
        pltpu.make_async_copy(a, b, load_sem.at[n])
        for n, (a, b) in enumerate(
            [(img, ext.at[3:7, 16:48]), (k1, k1v), (b1, b1v), (k2, k2v), (b2, b2v), (k3, k3v), (b3, b3v)]
        )
    ]
    for load in loads:
        load.start()

    for ds, dr in SIDES:
        z0, z1 = {-1: (0, 3), 0: (3, 7), 1: (7, 10)}[ds]
        y0, y1 = {-1: (0, 16), 0: (16, 48), 1: (48, 64)}[dr]

        @pl.when(~inside(ds, dr))
        def _():
            ext[z0:z1, y0:y1, :] = jnp.zeros((z1 - z0, y1 - y0, 128), BF16)

    for load in loads:
        load.wait()

    bias = b1v[...]
    high = bias.astype(BF16).astype(F32)
    mid = (bias - high).astype(BF16).astype(F32)
    low = bias - high - mid
    pieces = [k1v[a].astype(F32)[b : b + 1] for a in range(3) for b in range(3)] + [high, mid, low]
    row = iota((16, 32), 0)
    kk = jnp.zeros((16, 32), F32)
    for n, piece in enumerate(pieces):
        kk = jnp.where(row == n, jnp.broadcast_to(piece, (16, 32)), kk)
    kt = dot(kk.astype(BF16), spread(32, 512))

    def taps(height, lanes, b, first):
        out = jnp.zeros((height, lanes), F32)
        gap = iota((height, lanes), 0) - (iota((height, lanes), 1) >> 5) - first
        for a in range(3):
            n = 3 * a + b
            out = jnp.where(gap == a, jnp.broadcast_to(kt[n : n + 1, :lanes], (height, lanes)), out)
        return out

    def biases(out, first):
        height, lanes = out.shape
        at = iota((height, lanes), 0) - first
        for m in range(3):
            out = jnp.where(at == m, jnp.broadcast_to(kt[9 + m : 10 + m, :lanes], (height, lanes)), out)
        return out

    tall = jnp.concatenate(
        [taps(32, 512, b, 13) for b in range(3)] + [biases(jnp.zeros((32, 512), F32), 0)], axis=0
    )
    w1x[...] = tall.T.astype(BF16)
    flat = jnp.concatenate(
        [taps(16, 256, 0, 0), biases(taps(16, 256, 1, 0), 10), taps(16, 256, 2, 0), jnp.zeros((80, 256), F32)], axis=0
    )
    w1z[...] = flat.T[:, :48].astype(BF16)

    z_of = s * 4 + (iota((32, 256), 1) >> 5)
    in_two = (z_of >= 2) & (z_of < 4 * slabs + 2)
    part = iota((32, 256), 1) >> 5
    wide = dot(k2v[...].reshape(288, 32), spread(32, 256))
    for b in range(3):
        for o in range(6):
            block = jnp.zeros((32, 256), F32)
            for a in range(3):
                n = (3 * a + b) * 32
                block = jnp.where(part == o + a, wide[n : n + 32], block)
            w2x[o * 32 : o * 32 + 32, b * 256 : b * 256 + 256] = block.astype(BF16)
            w2z[o * 32 : o * 32 + 32, b * 256 : b * 256 + 256] = jnp.where(in_two, block, 0.0).astype(BF16)
    column = jnp.sum(
        jnp.where(iota((32, 32), 0) == iota((32, 32), 1), jnp.broadcast_to(b2v[...], (32, 32)), 0.0), axis=1, keepdims=True
    )
    for o in range(6):
        b2c[o * 32 : o * 32 + 32, :] = jnp.broadcast_to(column, (32, 128))

    group = iota((48, 32), 0) >> 2
    lasts = []
    for a in range(3):
        last = jnp.zeros((48, 32), F32)
        for b in range(3):
            line = k3v[a, b].astype(F32)
            for f in range(3):
                last = jnp.where(group == 4 * b + f, jnp.broadcast_to(line[f : f + 1], (48, 32)), last)
        lasts.append(last)
    wide3 = dot(jnp.concatenate(lasts, axis=0).astype(BF16), spread(32, 192))
    part3 = (iota((48, 192), 1) >> 5) - (iota((48, 192), 0) & 3)
    last = jnp.zeros((48, 192), F32)
    for a in range(3):
        last = jnp.where(part3 == a, wide3[48 * a : 48 * a + 48], last)
    z_of = s * 4 + (iota((48, 192), 1) >> 5)
    w3x[...] = last.astype(BF16)
    w3z[...] = jnp.where((z_of >= 1) & (z_of < 4 * slabs + 1), last, 0.0).astype(BF16)

    kind = iota((16, 128), 0) >> 2
    flow = [jnp.broadcast_to(b3v[0:1, f : f + 1], (16, 128)) for f in range(3)]
    brow[...] = jnp.where(kind == 0, flow[0], 0.0)
    bias_xy = jnp.where(kind == 0, 0.5 * (flow[0] + flow[1]), jnp.where(kind == 1, flow[1], flow[2]))
    scale_xy = jnp.where(kind == 1, 1.0, 0.5)

    def answer(ds, dr, extra=True):
        @pl.when(inside(ds, dr) & later(ds, dr) & extra)
        def _():
            copies[SIDES.index((-ds, -dr))].wait_recv()
            copies[SIDES.index((ds, dr))].start()

    def collect(ds, dr):
        @pl.when(inside(ds, dr) & ~later(ds, dr))
        def _():
            copies[SIDES.index((-ds, -dr))].wait_recv()

    answer(0, 1)
    for dr in (0, -1, 1):
        answer(1, dr)
    collect(0, -1)

    lane = iota((64, 128), 1)
    for z in range(4):
        plane = ext[3 + z].astype(F32)
        at = pl.ds(z * 128, 128)
        imx[0, :, at] = jnp.where(lane == 0, 0.0, pltpu.roll(plane, 1, 1)).astype(BF16)
        imx[1, :, at] = plane.astype(BF16)
        imx[2, :, at] = jnp.where(lane == 127, 0.0, pltpu.roll(plane, 127, 1)).astype(BF16)

    def shifted(values, by):
        edge = iota((values.shape[0], 128), 1) == (0 if by > 0 else 127)
        halves = [jnp.where(edge, 0.0, pltpu.roll(values[:, h : h + 128], by % 128, 1)) for h in (0, 128)]
        return jnp.concatenate(halves, axis=1)

    bias_two = jnp.concatenate([b2c[...]] * 2, axis=1)

    def pair(t, carry):
        cols = pl.ds(pl.multiple_of(t * 256, 256), 256)
        for j, height in ((0, 512), (1, 512), (2, 128)):
            window = [imx[b, 16 * j : 16 * j + 32, cols] for b in range(3)]
            rhs = jnp.concatenate(window + [jnp.ones((32, 256), BF16)], axis=0)
            hidden = jnp.maximum(dot(w1x[:height], rhs), 0.0)
            h1c[512 * j : 512 * j + height] = hidden.astype(BF16)
            h1l[512 * j : 512 * j + height] = shifted(hidden, 1).astype(BF16)
            h1r[512 * j : 512 * j + height] = shifted(hidden, -1).astype(BF16)

        for ref in (h1c, h1l, h1r):

            @pl.when(r == 0)
            def _():
                ref[:64] = jnp.zeros((64, 256), BF16)

            @pl.when(r == rows - 1)
            def _():
                ref[1088:] = jnp.zeros((64, 256), BF16)

        for first in (0, 6, 12, 18, 24, 28):
            at = first * 32
            rhs = jnp.concatenate([ref[at : at + 256] for ref in (h1l, h1c, h1r)], axis=0)
            h2x[at : at + 192] = jnp.maximum(dot(w2x[...], rhs) + bias_two, 0.0).astype(BF16)

        @pl.when(r == 0)
        def _():
            h2x[:32] = jnp.zeros((32, 256), BF16)

        @pl.when(r == rows - 1)
        def _():
            h2x[1056:] = jnp.zeros((32, 256), BF16)

        for k in range(8):
            terms = dot(w3x[...], h2x[128 * k : 128 * k + 192])
            total = shifted(terms[:16], 1) + terms[16:32] + shifted(terms[32:], -1)
            for h in range(2):
                flows = total[:, 128 * h : 128 * h + 128] * scale_xy + bias_xy
                for f in range(3):
                    xyp[pl.ds((4 * f + 2 * t + h) * 32 + 4 * k, 4), :] = flows[4 * f : 4 * f + 4]
        return carry

    lax.fori_loop(0, 2, pair, 0)

    for dr in (0, -1, 1):
        answer(-1, dr)
    for dr in (0, -1, 1):
        collect(1, dr)
        collect(-1, dr)
    for n, (ds, dr) in enumerate(SIDES):

        @pl.when(inside(ds, dr))
        def _():
            copies[n].wait_send()


def yz_kernel(ext, w1, w2, w3, b2c, brow, xyp, out, imt, h1, h2, p3):
    r = lax.axis_index("row")
    first = jnp.where(r == 0, 0.0, 1.0)
    final = jnp.where(r == lax.axis_size("row") - 1, 0.0, 1.0)

    for z in range(10):
        imt[pl.ds(z, 64, stride=16), :] = ext[z].astype(F32)
    for z in range(10, 16):
        imt[pl.ds(z, 64, stride=16), :] = jnp.ones((64, 128), F32)

    bias_two = jnp.concatenate([b2c[...]] * 2, axis=1)
    kind = iota((16, 128), 0) >> 2
    scale = jnp.where(kind == 0, 1.0, 0.5)
    add = brow[...]

    def one(j):
        rhs = jnp.concatenate([imt[(j + h + 13) * 16 : (j + h + 16) * 16, :].astype(BF16) for h in range(2)], axis=1)
        hidden = jnp.maximum(dot(w1[...], rhs), 0.0)
        if j == 0:
            hidden = hidden * first
        if j == 34:
            hidden = hidden * final
        h1[:, j * 128 : j * 128 + 256] = hidden.astype(BF16)

    def two(j):
        rhs = jnp.concatenate([h1[:, (j + b) * 128 : (j + b) * 128 + 256] for b in range(3)], axis=0)
        hidden = jnp.maximum(dot(w2[...], rhs) + bias_two, 0.0)
        if j == 0:
            hidden = jnp.concatenate([hidden[:, :128] * first, hidden[:, 128:]], axis=1)
        if j == 32:
            hidden = jnp.concatenate([hidden[:, :128], hidden[:, 128:] * final], axis=1)
        h2[:, j * 128 : j * 128 + 256] = hidden.astype(BF16)

    def three(j):
        p3[:, j * 128 : j * 128 + 256] = dot(w3[...], h2[:, j * 128 : j * 128 + 256])

    def finish(y):
        total = sum(p3[16 * b : 16 * b + 16, (y + b) * 128 : (y + b) * 128 + 128] for b in range(3))
        flows = total * scale + add
        out[pl.ds(y, 8, stride=32), :] = flows[:8]
        out[pl.ds(384 + y, 4, stride=32), :] = flows[8:12]

    for step in range(22):
        if step < 18:
            one(2 * step)
        if 2 <= step < 19:
            two(2 * (step - 2))
        if 3 <= step < 20:
            three(2 * (step - 3))
        if 5 <= step < 21:
            finish(2 * (step - 5))
            finish(2 * (step - 5) + 1)
    out[128:256, :] = out[128:256, :] + xyp[:128]
    out[256:384, :] = xyp[128:256]
    out[384:512, :] = out[384:512, :] + xyp[256:]


def local(image, first_kernel, first_bias, middle_kernel, middle_bias, last_kernel, last_bias):
    args = (
        image,
        first_kernel.reshape(3, 3, 32),
        first_bias.reshape(1, 32),
        middle_kernel,
        middle_bias.reshape(1, 32),
        last_kernel,
        last_bias.reshape(1, 3),
    )
    args = [pltpu.with_memory_space_constraint(a, pltpu.HBM) for a in args]
    shape = jax.ShapeDtypeStruct
    vmem = pl.BlockSpec(memory_space=pltpu.VMEM)
    outs = [
        shape((10, 64, 128), BF16),
        shape((256, 48), BF16),
        shape((192, 768), BF16),
        shape((48, 192), BF16),
        shape((192, 128), F32),
        shape((16, 128), F32),
        shape((384, 128), F32),
    ]
    made = pl.pallas_call(
        exchange_kernel,
        out_shape=outs,
        in_specs=[pl.BlockSpec(memory_space=pltpu.HBM)] * 7,
        out_specs=[vmem] * 7,
        scratch_shapes=[
            pltpu.VMEM((3, 3, 32), BF16),
            pltpu.VMEM((1, 32), F32),
            pltpu.VMEM((3, 3, 32, 32), BF16),
            pltpu.VMEM((1, 32), F32),
            pltpu.VMEM((3, 3, 3, 32), BF16),
            pltpu.VMEM((1, 3), F32),
            pltpu.VMEM((512, 128), BF16),
            pltpu.VMEM((192, 768), BF16),
            pltpu.VMEM((48, 192), BF16),
            pltpu.VMEM((3, 64, 512), BF16),
            pltpu.VMEM((1152, 256), BF16),
            pltpu.VMEM((1152, 256), BF16),
            pltpu.VMEM((1152, 256), BF16),
            pltpu.VMEM((1088, 256), BF16),
            pltpu.SemaphoreType.DMA((7,)),
            pltpu.SemaphoreType.DMA((8,)),
            pltpu.SemaphoreType.DMA((8,)),
        ],
        compiler_params=pltpu.CompilerParams(collective_id=0, has_side_effects=True, vmem_limit_bytes=24 * 2**20),
    )(*args)
    flows = pl.pallas_call(
        yz_kernel,
        out_shape=shape((512, 128), F32),
        in_specs=[vmem] * 7,
        out_specs=vmem,
        scratch_shapes=[
            pltpu.VMEM((1024, 128), F32),
            pltpu.VMEM((256, 36 * 128), BF16),
            pltpu.VMEM((192, 34 * 128), BF16),
            pltpu.VMEM((48, 34 * 128), F32),
        ],
        compiler_params=pltpu.CompilerParams(vmem_limit_bytes=24 * 2**20),
    )(*made)
    return flows.reshape(4, 4, 32, 128)


def solution(mesh):
    placed = (P("slab", "row", None), P(), P(), P(), P(), P(), P())
    return jax.shard_map(
        local, mesh=mesh, in_specs=placed, out_specs=P(None, "slab", "row", None), check_vma=False
    )
```

```python
import jax
import jax.numpy as jnp
from jax import lax
from jax.experimental import pallas as pl
from jax.experimental.pallas import tpu as pltpu
from jax.sharding import PartitionSpec as P

MESH = pl.DeviceIdType.MESH
F32 = jnp.float32
BF16 = jnp.bfloat16

SIDES = [(ds, dr) for ds in (1, -1, 0) for dr in (0, 1, -1) if ds or dr]
RUN = 32


def iota(shape, dim):
    return lax.broadcasted_iota(jnp.int32, shape, dim)


def spread(rows, lanes):
    return ((iota((rows, lanes), 1) & 31) == iota((rows, lanes), 0)).astype(BF16)


def dot(a, b):
    return jnp.dot(a, b, preferred_element_type=F32)


def span(step, own, low, high):
    return {0: own, 1: low, -1: high}[step]


def kernel(
    img, k1, b1, k2, b2, k3, b3,
    out,
    ext, w1z, w2z, w3z, b2c, xyp, imt, g1, g2, p3,
    k1v, b1v, k2v, b2v, k3v, b3v, w1x, w2x, w3x, imx, h1c, h1l, h1r, h2x,
    load_sem, send_sem, recv_sem,
):
    s = lax.axis_index("slab")
    r = lax.axis_index("row")
    slabs = lax.axis_size("slab")
    rows = lax.axis_size("row")
    place = lax.rem(s, RUN)
    wrap = place == RUN - 1

    def inside(ds, dr):
        return (s + ds >= 0) & (s + ds < slabs) & (r + dr >= 0) & (r + dr < rows)

    def uneven(ds):
        return wrap if ds == 0 else (wrap | (place == RUN - 2) if ds > 0 else wrap | (place == 0))

    def first(ds, dr):
        if ds == 0:
            return (r ^ 1) < ((r + dr) ^ 1)
        if ds > 0:
            return jnp.bool_(False)
        return jnp.bool_(True)

    barrier = pltpu.get_barrier_semaphore()
    greeted = jnp.int32(0)
    for ds, dr in SIDES:
        greeted += (inside(ds, dr) & ~(uneven(ds) & first(ds, dr))).astype(jnp.int32)

    def greet(ds, dr):
        @pl.when(inside(ds, dr) & ~(uneven(ds) & ~first(ds, dr)))
        def _():
            pl.semaphore_signal(barrier, inc=1, device_id=(s + ds, r + dr), device_id_type=MESH)

    copies = {}
    for n, (ds, dr) in enumerate(SIDES):
        zs, zd = span(ds, ((0, 4), (3, 7)), ((1, 4), (0, 3)), ((0, 3), (7, 10)))
        ys, yd = span(dr, ((0, 32), (16, 48)), ((16, 32), (0, 16)), ((0, 16), (48, 64)))
        copies[ds, dr] = pltpu.make_async_remote_copy(
            src_ref=img.at[zs[0] : zs[1], ys[0] : ys[1]],
            dst_ref=ext.at[zd[0] : zd[1], yd[0] : yd[1]],
            send_sem=send_sem.at[n],
            recv_sem=recv_sem.at[n],
            device_id=(s + ds, r + dr),
            device_id_type=MESH,
        )

    broad = pltpu.make_async_remote_copy(
        src_ref=ext.at[3:6],
        dst_ref=ext.at[7:10],
        send_sem=send_sem.at[8],
        recv_sem=recv_sem.at[8],
        device_id=(s - 1, r),
        device_id_type=MESH,
    )
    head = (place == 0) & (s > 0)
    tail = wrap & (s < slabs - 1)

    def meet_and_send():
        @pl.when(greeted > 0)
        def _():
            pl.semaphore_wait(barrier, greeted)

        for ds, dr in SIDES:

            @pl.when(inside(ds, dr) & ~(uneven(ds) & first(ds, dr)))
            def _():
                copies[ds, dr].start()

    def arrive(ds, dr):
        @pl.when(inside(ds, dr))
        def _():
            copies[-ds, -dr].wait_recv()

        @pl.when(inside(ds, dr) & uneven(ds) & first(ds, dr))
        def _():
            copies[ds, dr].start()

    def arrive_head(dr):
        @pl.when(head & inside(-1, dr))
        def _():
            copies[1, -dr].wait_recv()
            if dr == 0:
                broad.start()

    greet(0, 1)
    greet(0, -1)

    @pl.when(wrap)
    def _():
        meet_and_send()

    for ds in (1, -1):
        for dr in (0, 1, -1):
            greet(ds, dr)

    loads = [
        pltpu.make_async_copy(a, b, load_sem.at[n])
        for n, (a, b) in enumerate(
            [(img, ext.at[3:7, 16:48]), (k1, k1v), (b1, b1v), (k2, k2v), (b2, b2v), (k3, k3v), (b3, b3v)]
        )
    ]
    for load in loads:
        load.start()

    for ds, dr in SIDES:
        z0, z1 = {-1: (0, 3), 0: (3, 7), 1: (7, 10)}[ds]
        y0, y1 = {-1: (0, 16), 0: (16, 48), 1: (48, 64)}[dr]

        @pl.when(~inside(ds, dr) & ~(tail if ds == 1 else jnp.bool_(False)))
        def _():
            ext[z0:z1, y0:y1, :] = jnp.zeros((z1 - z0, y1 - y0, 128), BF16)

    for z in range(10, 16):
        imt[pl.ds(z, 64, stride=16), :] = jnp.ones((64, 128), F32)
    for load in loads:
        load.wait()

    bias = b1v[...]
    high = bias.astype(BF16).astype(F32)
    mid = (bias - high).astype(BF16).astype(F32)
    low = bias - high - mid
    pieces = [k1v[a].astype(F32)[b : b + 1] for a in range(3) for b in range(3)] + [high, mid, low]
    row = iota((16, 32), 0)
    kk = jnp.zeros((16, 32), F32)
    for n, piece in enumerate(pieces):
        kk = jnp.where(row == n, jnp.broadcast_to(piece, (16, 32)), kk)
    kt = dot(kk.astype(BF16), spread(32, 512))

    def taps(height, lanes, b, first):
        out = jnp.zeros((height, lanes), F32)
        gap = iota((height, lanes), 0) - (iota((height, lanes), 1) >> 5) - first
        for a in range(3):
            n = 3 * a + b
            out = jnp.where(gap == a, jnp.broadcast_to(kt[n : n + 1, :lanes], (height, lanes)), out)
        return out

    def biases(out, first):
        height, lanes = out.shape
        at = iota((height, lanes), 0) - first
        for m in range(3):
            out = jnp.where(at == m, jnp.broadcast_to(kt[9 + m : 10 + m, :lanes], (height, lanes)), out)
        return out

    tall = jnp.concatenate(
        [taps(32, 512, b, 13) for b in range(3)] + [biases(jnp.zeros((32, 512), F32), 0)], axis=0
    )
    w1x[...] = tall.T.astype(BF16)
    flat = jnp.concatenate(
        [taps(16, 256, 0, 0), biases(taps(16, 256, 1, 0), 10), taps(16, 256, 2, 0), jnp.zeros((80, 256), F32)], axis=0
    )
    w1z[...] = flat.T[:, :48].astype(BF16)

    z_of = s * 4 + (iota((32, 256), 1) >> 5)
    in_two = (z_of >= 2) & (z_of < 4 * slabs + 2)
    part = iota((32, 256), 1) >> 5
    wide = dot(k2v[...].reshape(288, 32), spread(32, 256))
    for b in range(3):
        for o in range(6):
            block = jnp.zeros((32, 256), F32)
            for a in range(3):
                n = (3 * a + b) * 32
                block = jnp.where(part == o + a, wide[n : n + 32], block)
            w2x[o * 32 : o * 32 + 32, b * 256 : b * 256 + 256] = block.astype(BF16)
            w2z[o * 32 : o * 32 + 32, b * 256 : b * 256 + 256] = jnp.where(in_two, block, 0.0).astype(BF16)
    column = jnp.sum(
        jnp.where(iota((32, 32), 0) == iota((32, 32), 1), jnp.broadcast_to(b2v[...], (32, 32)), 0.0), axis=1, keepdims=True
    )
    for o in range(6):
        b2c[o * 32 : o * 32 + 32, :] = jnp.broadcast_to(column, (32, 128))

    group = iota((48, 32), 0) >> 2
    lasts = []
    for a in range(3):
        last = jnp.zeros((48, 32), F32)
        for b in range(3):
            line = k3v[a, b].astype(F32)
            for f in range(3):
                last = jnp.where(group == 4 * b + f, jnp.broadcast_to(line[f : f + 1], (48, 32)), last)
        lasts.append(last)
    wide3 = dot(jnp.concatenate(lasts, axis=0).astype(BF16), spread(32, 192))
    part3 = (iota((48, 192), 1) >> 5) - (iota((48, 192), 0) & 3)
    last = jnp.zeros((48, 192), F32)
    for a in range(3):
        last = jnp.where(part3 == a, wide3[48 * a : 48 * a + 48], last)
    z_of = s * 4 + (iota((48, 192), 1) >> 5)
    w3x[...] = last.astype(BF16)
    w3z[...] = jnp.where((z_of >= 1) & (z_of < 4 * slabs + 1), last, 0.0).astype(BF16)

    kind = iota((16, 128), 0) >> 2
    flow = [jnp.broadcast_to(b3v[0:1, f : f + 1], (16, 128)) for f in range(3)]
    bias_yz = jnp.where(kind == 0, flow[0], 0.0)
    scale_yz = jnp.where(kind == 0, 1.0, 0.5)
    bias_xy = jnp.where(kind == 0, 0.5 * (flow[0] + flow[1]), jnp.where(kind == 1, flow[1], flow[2]))
    scale_xy = jnp.where(kind == 1, 1.0, 0.5)

    @pl.when(~wrap)
    def _():
        meet_and_send()

    arrive(0, 1)
    arrive(0, -1)

    @pl.when(wrap)
    def _():
        for dr in (0, 1, -1):
            arrive(-1, dr)

    lane = iota((64, 128), 1)
    for z in range(4):
        plane = ext[3 + z].astype(F32)
        at = pl.ds(z * 128, 128)
        imx[0, :, at] = jnp.where(lane == 0, 0.0, pltpu.roll(plane, 1, 1)).astype(BF16)
        imx[1, :, at] = plane.astype(BF16)
        imx[2, :, at] = jnp.where(lane == 127, 0.0, pltpu.roll(plane, 127, 1)).astype(BF16)

    def shifted(values, by):
        edge = iota((values.shape[0], 128), 1) == (0 if by > 0 else 127)
        halves = [jnp.where(edge, 0.0, pltpu.roll(values[:, h : h + 128], by % 128, 1)) for h in (0, 128)]
        return jnp.concatenate(halves, axis=1)

    bias_two = jnp.concatenate([b2c[...]] * 2, axis=1)

    def pair(t, carry):
        cols = pl.ds(pl.multiple_of(t * 256, 256), 256)
        for j, height in ((0, 512), (1, 512), (2, 128)):
            window = [imx[b, 16 * j : 16 * j + 32, cols] for b in range(3)]
            rhs = jnp.concatenate(window + [jnp.ones((32, 256), BF16)], axis=0)
            hidden = jnp.maximum(dot(w1x[:height], rhs), 0.0)
            h1c[512 * j : 512 * j + height] = hidden.astype(BF16)
            h1l[512 * j : 512 * j + height] = shifted(hidden, 1).astype(BF16)
            h1r[512 * j : 512 * j + height] = shifted(hidden, -1).astype(BF16)

        for ref in (h1c, h1l, h1r):

            @pl.when(r == 0)
            def _():
                ref[:64] = jnp.zeros((64, 256), BF16)

            @pl.when(r == rows - 1)
            def _():
                ref[1088:] = jnp.zeros((64, 256), BF16)

        for first in (0, 6, 12, 18, 24, 28):
            at = first * 32
            rhs = jnp.concatenate([ref[at : at + 256] for ref in (h1l, h1c, h1r)], axis=0)
            h2x[at : at + 192] = jnp.maximum(dot(w2x[...], rhs) + bias_two, 0.0).astype(BF16)

        @pl.when(r == 0)
        def _():
            h2x[:32] = jnp.zeros((32, 256), BF16)

        @pl.when(r == rows - 1)
        def _():
            h2x[1056:] = jnp.zeros((32, 256), BF16)

        for k in range(8):
            terms = dot(w3x[...], h2x[128 * k : 128 * k + 192])
            total = shifted(terms[:16], 1) + terms[16:32] + shifted(terms[32:], -1)
            for h in range(2):
                flows = total[:, 128 * h : 128 * h + 128] * scale_xy + bias_xy
                for f in range(3):
                    xyp[pl.ds((4 * f + 2 * t + h) * 32 + 4 * k, 4), :] = flows[4 * f : 4 * f + 4]
        return carry

    lax.fori_loop(0, 2, pair, 0)

    def turn(z0, z1, y0, y1):
        for z in range(z0, z1):
            imt[pl.ds(16 * y0 + z, y1 - y0, stride=16), :] = ext[z, y0:y1, :].astype(F32)

    def arrive_high(dr):
        @pl.when(~wrap)
        def _():
            arrive(1, dr)

    def arrive_low(dr):
        @pl.when(~wrap & ~head)
        def _():
            arrive(-1, dr)

    turn(3, 7, 0, 64)
    arrive_high(0)
    arrive_high(-1)

    @pl.when(tail)
    def _():
        broad.wait_recv()

    turn(7, 10, 0, 48)
    arrive_low(0)
    arrive_low(-1)
    arrive_head(0)
    arrive_head(-1)
    turn(0, 3, 0, 48)

    top = jnp.where(r == 0, 0.0, 1.0)
    bottom = jnp.where(r == rows - 1, 0.0, 1.0)

    def one(j):
        rhs = jnp.concatenate([imt[(j + h + 13) * 16 : (j + h + 16) * 16, :].astype(BF16) for h in range(2)], axis=1)
        hidden = jnp.maximum(dot(w1z[...], rhs), 0.0)
        if j == 0:
            hidden = hidden * top
        if j == 34:
            hidden = hidden * bottom
        g1[:, j * 128 : j * 128 + 256] = hidden.astype(BF16)

    def two(j):
        rhs = jnp.concatenate([g1[:, (j + b) * 128 : (j + b) * 128 + 256] for b in range(3)], axis=0)
        hidden = jnp.maximum(dot(w2z[...], rhs) + bias_two, 0.0)
        if j == 0:
            hidden = jnp.concatenate([hidden[:, :128] * top, hidden[:, 128:]], axis=1)
        if j == 32:
            hidden = jnp.concatenate([hidden[:, :128], hidden[:, 128:] * bottom], axis=1)
        g2[:, j * 128 : j * 128 + 256] = hidden.astype(BF16)

    def three(j):
        p3[:, j * 128 : j * 128 + 256] = dot(w3z[...], g2[:, j * 128 : j * 128 + 256])

    def finish(y):
        total = sum(p3[16 * b : 16 * b + 16, (y + b) * 128 : (y + b) * 128 + 128] for b in range(3))
        flows = total * scale_yz + bias_yz
        out[pl.ds(y, 8, stride=32), :] = flows[:8]
        out[pl.ds(384 + y, 4, stride=32), :] = flows[8:12]

    for k in range(16):
        one(2 * k)
    for k in range(15):
        two(2 * k)
    for k in range(15):
        three(2 * k)
    for y in range(28):
        finish(y)
    arrive_high(1)
    turn(7, 10, 48, 64)
    arrive_low(1)
    arrive_head(1)
    turn(0, 3, 48, 64)
    for k in range(16, 18):
        one(2 * k)
    for k in range(15, 17):
        two(2 * k)
    for k in range(15, 17):
        three(2 * k)
    for y in range(28, 32):
        finish(y)
    out[128:256, :] = out[128:256, :] + xyp[:128]
    out[256:384, :] = xyp[128:256]
    out[384:512, :] = out[384:512, :] + xyp[256:]

    for ds, dr in SIDES:

        @pl.when(inside(ds, dr) & ~(head if ds == -1 else jnp.bool_(False)))
        def _():
            copies[ds, dr].wait_send()

    @pl.when(head)
    def _():
        broad.wait_send()


def local(image, first_kernel, first_bias, middle_kernel, middle_bias, last_kernel, last_bias):
    args = (
        image,
        first_kernel.reshape(3, 3, 32),
        first_bias.reshape(1, 32),
        middle_kernel,
        middle_bias.reshape(1, 32),
        last_kernel,
        last_bias.reshape(1, 3),
    )
    args = [pltpu.with_memory_space_constraint(a, pltpu.HBM) for a in args]
    shape = jax.ShapeDtypeStruct
    vmem = pl.BlockSpec(memory_space=pltpu.VMEM)
    flows = pl.pallas_call(
        kernel,
        out_shape=shape((512, 128), F32),
        in_specs=[pl.BlockSpec(memory_space=pltpu.HBM)] * 7,
        out_specs=vmem,
        scratch_shapes=[
            pltpu.VMEM((10, 64, 128), BF16),
            pltpu.VMEM((256, 48), BF16),
            pltpu.VMEM((192, 768), BF16),
            pltpu.VMEM((48, 192), BF16),
            pltpu.VMEM((192, 128), F32),
            pltpu.VMEM((384, 128), F32),
            pltpu.VMEM((1024, 128), F32),
            pltpu.VMEM((256, 36 * 128), BF16),
            pltpu.VMEM((192, 34 * 128), BF16),
            pltpu.VMEM((48, 34 * 128), F32),
            pltpu.VMEM((3, 3, 32), BF16),
            pltpu.VMEM((1, 32), F32),
            pltpu.VMEM((3, 3, 32, 32), BF16),
            pltpu.VMEM((1, 32), F32),
            pltpu.VMEM((3, 3, 3, 32), BF16),
            pltpu.VMEM((1, 3), F32),
            pltpu.VMEM((512, 128), BF16),
            pltpu.VMEM((192, 768), BF16),
            pltpu.VMEM((48, 192), BF16),
            pltpu.VMEM((3, 64, 512), BF16),
            pltpu.VMEM((1152, 256), BF16),
            pltpu.VMEM((1152, 256), BF16),
            pltpu.VMEM((1152, 256), BF16),
            pltpu.VMEM((1088, 256), BF16),
            pltpu.SemaphoreType.DMA((7,)),
            pltpu.SemaphoreType.DMA((9,)),
            pltpu.SemaphoreType.DMA((9,)),
        ],
        compiler_params=pltpu.CompilerParams(collective_id=0, has_side_effects=True, vmem_limit_bytes=24 * 2**20),
    )(*args)
    return flows.reshape(4, 4, 32, 128)


def solution(mesh):
    placed = (P("slab", "row", None), P(), P(), P(), P(), P(), P())
    return jax.shard_map(
        local, mesh=mesh, in_specs=placed, out_specs=P(None, "slab", "row", None), check_vma=False
    )
```

```python
import jax
import jax.numpy as jnp
from jax import lax
from jax.experimental import pallas as pl
from jax.experimental.pallas import tpu as pltpu
from jax.sharding import PartitionSpec as P

MESH = pl.DeviceIdType.MESH
F32 = jnp.float32
BF16 = jnp.bfloat16

SIDES = [(ds, dr) for ds in (1, -1, 0) for dr in (-1, 0, 1) if ds or dr]
RUN = 32


def iota(shape, dim):
    return lax.broadcasted_iota(jnp.int32, shape, dim)


def spread(rows, lanes):
    return ((iota((rows, lanes), 1) & 31) == iota((rows, lanes), 0)).astype(BF16)


def dot(a, b):
    return jnp.dot(a, b, preferred_element_type=F32)


def span(step, own, low, high):
    return {0: own, 1: low, -1: high}[step]


def kernel(
    img, k1, b1, k2, b2, k3, b3,
    out,
    ext, w1z, w2z, w3z, b2c, xyp, imt, g1, g2, p3,
    k1v, b1v, k2v, b2v, k3v, b3v, w1x, w2x, w3x, imx, h1c, h1l, h1r, h2x,
    load_sem, send_sem, recv_sem,
):
    s = lax.axis_index("slab")
    r = lax.axis_index("row")
    slabs = lax.axis_size("slab")
    rows = lax.axis_size("row")
    place = lax.rem(s, RUN)
    wrap = (place == RUN - 1) & (s < slabs - 1)

    def inside(ds, dr):
        return (s + ds >= 0) & (s + ds < slabs) & (r + dr >= 0) & (r + dr < rows)

    def greets(ds):
        return wrap | (place == 0) if ds < 0 else jnp.bool_(False)

    def greeted_by(ds):
        return wrap | ((place == RUN - 2) & (s < slabs - 2)) if ds > 0 else jnp.bool_(False)

    def aside(ds):
        return wrap if ds == 0 else jnp.bool_(False)

    barrier = pltpu.get_barrier_semaphore()
    greeted = jnp.int32(0)
    for ds, dr in SIDES:
        greeted += (inside(ds, dr) & ~greets(ds) & ~aside(ds)).astype(jnp.int32)

    def greet(ds, dr):
        @pl.when(inside(ds, dr) & ~greeted_by(ds) & ~aside(ds))
        def _():
            pl.semaphore_signal(barrier, inc=1, device_id=(s + ds, r + dr), device_id_type=MESH)

    copies = {}
    for n, (ds, dr) in enumerate(SIDES):
        zs, zd = span(ds, ((0, 4), (3, 7)), ((1, 4), (0, 3)), ((0, 3), (7, 10)))
        ys, yd = span(dr, ((0, 32), (16, 48)), ((16, 32), (0, 16)), ((0, 16), (48, 64)))
        copies[ds, dr] = pltpu.make_async_remote_copy(
            src_ref=img.at[zs[0] : zs[1], ys[0] : ys[1]],
            dst_ref=ext.at[zd[0] : zd[1], yd[0] : yd[1]],
            send_sem=send_sem.at[n],
            recv_sem=recv_sem.at[n],
            device_id=(s + ds, r + dr),
            device_id_type=MESH,
        )

    broad = pltpu.make_async_remote_copy(
        src_ref=ext.at[3:6],
        dst_ref=ext.at[7:10],
        send_sem=send_sem.at[8],
        recv_sem=recv_sem.at[8],
        device_id=(s - 1, r),
        device_id_type=MESH,
    )
    head = (place == 0) & (s > 0)

    def meet_and_send():
        @pl.when(greeted > 0)
        def _():
            pl.semaphore_wait(barrier, greeted)

        for ds, dr in SIDES:

            @pl.when(inside(ds, dr) & ~greets(ds) & ~aside(ds))
            def _():
                copies[ds, dr].start()

    def arrive(ds, dr):
        @pl.when(inside(ds, dr))
        def _():
            copies[-ds, -dr].wait_recv()

        @pl.when(inside(ds, dr) & greets(ds))
        def _():
            copies[ds, dr].start()

    def arrive_head(dr):
        @pl.when(head & inside(-1, dr))
        def _():
            copies[1, -dr].wait_recv()
            if dr == 0:
                broad.start()

    greet(0, 1)
    greet(0, -1)

    @pl.when(wrap)
    def _():
        meet_and_send()

    for ds in (1, -1):
        for dr in (0, 1, -1):
            greet(ds, dr)

    loads = [
        pltpu.make_async_copy(a, b, load_sem.at[n])
        for n, (a, b) in enumerate(
            [(img, ext.at[3:7, 16:48]), (k1, k1v), (b1, b1v), (k2, k2v), (b2, b2v), (k3, k3v), (b3, b3v)]
        )
    ]
    for load in loads:
        load.start()

    for ds, dr in SIDES:
        z0, z1 = {-1: (0, 3), 0: (3, 7), 1: (7, 10)}[ds]
        y0, y1 = {-1: (0, 16), 0: (16, 48), 1: (48, 64)}[dr]

        @pl.when(~inside(ds, dr) & ~(wrap if ds == 1 else jnp.bool_(False)))
        def _():
            ext[z0:z1, y0:y1, :] = jnp.zeros((z1 - z0, y1 - y0, 128), BF16)

    for z in range(10, 16):
        imt[pl.ds(z, 64, stride=16), :] = jnp.ones((64, 128), F32)
    for z in range(10):
        imt[pl.ds(z, 64, stride=16), :] = jnp.zeros((64, 128), F32)
    for load in loads:
        load.wait()

    bias = b1v[...]
    high = bias.astype(BF16).astype(F32)
    mid = (bias - high).astype(BF16).astype(F32)
    low = bias - high - mid
    pieces = [k1v[a].astype(F32)[b : b + 1] for a in range(3) for b in range(3)] + [high, mid, low]
    row = iota((16, 32), 0)
    kk = jnp.zeros((16, 32), F32)
    for n, piece in enumerate(pieces):
        kk = jnp.where(row == n, jnp.broadcast_to(piece, (16, 32)), kk)
    kt = dot(kk.astype(BF16), spread(32, 512))

    def taps(height, lanes, b, first):
        out = jnp.zeros((height, lanes), F32)
        gap = iota((height, lanes), 0) - (iota((height, lanes), 1) >> 5) - first
        for a in range(3):
            n = 3 * a + b
            out = jnp.where(gap == a, jnp.broadcast_to(kt[n : n + 1, :lanes], (height, lanes)), out)
        return out

    def biases(out, first):
        height, lanes = out.shape
        at = iota((height, lanes), 0) - first
        for m in range(3):
            out = jnp.where(at == m, jnp.broadcast_to(kt[9 + m : 10 + m, :lanes], (height, lanes)), out)
        return out

    tall = jnp.concatenate(
        [taps(32, 512, b, 13) for b in range(3)] + [biases(jnp.zeros((32, 512), F32), 0)], axis=0
    )
    w1x[...] = tall.T.astype(BF16)
    flat = jnp.concatenate(
        [taps(16, 256, 0, 0), biases(taps(16, 256, 1, 0), 10), taps(16, 256, 2, 0), jnp.zeros((80, 256), F32)], axis=0
    )
    w1z[...] = flat.T[:, :48].astype(BF16)

    lane = iota((32, 480), 1)
    wide = sum(
        dot(
            k2v[:, b].reshape(96, 32),
            ((lane >= 160 * b) & (lane < 160 * b + 160) & ((lane & 31) == iota((32, 480), 0))).astype(BF16),
        )
        for b in range(3)
    )
    part = (lane - jnp.where(lane >= 320, 320, jnp.where(lane >= 160, 160, 0))) >> 5

    def in_two(skip):
        z = s * 4 - 2 + skip + part
        return (z >= 0) & (z < 4 * slabs)

    for o in range(3):
        block = jnp.zeros((32, 480), F32)
        for a in range(3):
            block = jnp.where(part == o + a, wide[a * 32 : a * 32 + 32], block)
        w2x[o * 32 : o * 32 + 32, :] = block.astype(BF16)
        for h, skip in ((0, 0), (1, 3)):
            w2z[h, o * 32 : o * 32 + 32, :] = jnp.where(in_two(skip), block, 0.0).astype(BF16)
    column = jnp.sum(
        jnp.where(iota((32, 32), 0) == iota((32, 32), 1), jnp.broadcast_to(b2v[...], (32, 32)), 0.0), axis=1, keepdims=True
    )
    for o in range(3):
        b2c[o * 32 : o * 32 + 32, :] = jnp.broadcast_to(column, (32, 128))

    group = iota((48, 32), 0) >> 2
    lasts = []
    for a in range(3):
        last = jnp.zeros((48, 32), F32)
        for b in range(3):
            line = k3v[a, b].astype(F32)
            for f in range(3):
                last = jnp.where(group == 4 * b + f, jnp.broadcast_to(line[f : f + 1], (48, 32)), last)
        lasts.append(last)
    wide3 = dot(jnp.concatenate(lasts, axis=0).astype(BF16), spread(32, 192))
    part3 = (iota((48, 192), 1) >> 5) - (iota((48, 192), 0) & 3)
    last = jnp.zeros((48, 192), F32)
    for a in range(3):
        last = jnp.where(part3 == a, wide3[48 * a : 48 * a + 48], last)
    z_of = s * 4 + (iota((48, 192), 1) >> 5)
    w3x[...] = last.astype(BF16)
    w3z[...] = jnp.where((z_of >= 1) & (z_of < 4 * slabs + 1), last, 0.0).astype(BF16)

    kind = iota((16, 128), 0) >> 2
    flow = [jnp.broadcast_to(b3v[0:1, f : f + 1], (16, 128)) for f in range(3)]
    bias_yz = jnp.where(kind == 0, flow[0], 0.0)
    scale_yz = jnp.where(kind == 0, 1.0, 0.5)
    bias_xy = jnp.where(kind == 0, 0.5 * (flow[0] + flow[1]), jnp.where(kind == 1, flow[1], flow[2]))
    scale_xy = jnp.where(kind == 1, 1.0, 0.5)

    @pl.when(~wrap)
    def _():
        meet_and_send()

    @pl.when(wrap)
    def _():
        arrive(-1, 0)
        for dr in (1, -1):

            @pl.when(inside(0, dr))
            def _():
                copies[0, dr].start()

        arrive(-1, 1)
        arrive(-1, -1)

    arrive(0, 1)
    arrive(0, -1)

    lane = iota((64, 128), 1)
    for z in range(4):
        plane = ext[3 + z].astype(F32)
        at = pl.ds(z * 128, 128)
        imx[0, :, at] = jnp.where(lane == 0, 0.0, pltpu.roll(plane, 1, 1)).astype(BF16)
        imx[1, :, at] = plane.astype(BF16)
        imx[2, :, at] = jnp.where(lane == 127, 0.0, pltpu.roll(plane, 127, 1)).astype(BF16)

    def shifted(values, by):
        edge = iota((values.shape[0], 128), 1) == (0 if by > 0 else 127)
        halves = [jnp.where(edge, 0.0, pltpu.roll(values[:, h : h + 128], by % 128, 1)) for h in (0, 128)]
        return jnp.concatenate(halves, axis=1)

    bias_two = jnp.concatenate([b2c[...]] * 2, axis=1)

    def pair(t, carry):
        cols = pl.ds(pl.multiple_of(t * 256, 256), 256)
        for j, height in ((0, 512), (1, 512), (2, 128)):
            window = [imx[b, 16 * j : 16 * j + 32, cols] for b in range(3)]
            rhs = jnp.concatenate(window + [jnp.ones((32, 256), BF16)], axis=0)
            hidden = jnp.maximum(dot(w1x[:height], rhs), 0.0)
            h1c[512 * j : 512 * j + height] = hidden.astype(BF16)
            h1l[512 * j : 512 * j + height] = shifted(hidden, 1).astype(BF16)
            h1r[512 * j : 512 * j + height] = shifted(hidden, -1).astype(BF16)

        for ref in (h1c, h1l, h1r):

            @pl.when(r == 0)
            def _():
                ref[:64] = jnp.zeros((64, 256), BF16)

            @pl.when(r == rows - 1)
            def _():
                ref[1088:] = jnp.zeros((64, 256), BF16)

        for start in (0, 3, 6, 9, 12, 15, 18, 21, 24, 27, 30, 31):
            at = start * 32
            rhs = jnp.concatenate([ref[at : at + 160] for ref in (h1l, h1c, h1r)], axis=0)
            h2x[at : at + 96] = jnp.maximum(dot(w2x[...], rhs) + bias_two, 0.0).astype(BF16)

        @pl.when(r == 0)
        def _():
            h2x[:32] = jnp.zeros((32, 256), BF16)

        @pl.when(r == rows - 1)
        def _():
            h2x[1056:] = jnp.zeros((32, 256), BF16)

        for k in range(8):
            terms = dot(w3x[...], h2x[128 * k : 128 * k + 192])
            total = shifted(terms[:16], 1) + terms[16:32] + shifted(terms[32:], -1)
            for h in range(2):
                flows = total[:, 128 * h : 128 * h + 128] * scale_xy + bias_xy
                for f in range(3):
                    xyp[pl.ds((4 * f + 2 * t + h) * 32 + 4 * k, 4), :] = flows[4 * f : 4 * f + 4]
        return carry

    lax.fori_loop(0, 2, pair, 0)

    def turn(z0, z1, y0, y1):
        for z in range(z0, z1):
            imt[pl.ds(16 * y0 + z, y1 - y0, stride=16), :] = ext[z, y0:y1, :].astype(F32)

    def arrive_high(dr):
        @pl.when(~wrap)
        def _():
            arrive(1, dr)

    def arrive_low(dr):
        @pl.when(~wrap & ~head)
        def _():
            arrive(-1, dr)

    top = jnp.where(r == 0, 0.0, 1.0)
    bottom = jnp.where(r == rows - 1, 0.0, 1.0)

    part_one = ((0, 96), (96, 256))

    def one(h, j):
        lo, hi = part_one[h]
        rhs = jnp.concatenate([imt[(j + i + 13) * 16 : (j + i + 16) * 16, :].astype(BF16) for i in range(2)], axis=1)
        hidden = jnp.maximum(dot(w1z[lo:hi], rhs), 0.0)
        if j == 0:
            hidden = hidden * top
        if j == 34:
            hidden = hidden * bottom
        g1[lo:hi, j * 128 : j * 128 + 256] = hidden.astype(BF16)

    def two(h, j):
        at = 96 * h
        rhs = jnp.concatenate([g1[at : at + 160, (j + b) * 128 : (j + b) * 128 + 256] for b in range(3)], axis=0)
        hidden = jnp.maximum(dot(w2z[h], rhs) + bias_two, 0.0)
        if j == 0:
            hidden = jnp.concatenate([hidden[:, :128] * top, hidden[:, 128:]], axis=1)
        if j == 32:
            hidden = jnp.concatenate([hidden[:, :128], hidden[:, 128:] * bottom], axis=1)
        g2[at : at + 96, j * 128 : j * 128 + 256] = hidden.astype(BF16)

    def three(j):
        p3[:, j * 128 : j * 128 + 256] = dot(w3z[...], g2[:, j * 128 : j * 128 + 256])

    def finish(y):
        total = sum(p3[16 * b : 16 * b + 16, (y + b) * 128 : (y + b) * 128 + 128] for b in range(3))
        flows = total * scale_yz + bias_yz
        out[pl.ds(y, 8, stride=32), :] = flows[:8]
        out[pl.ds(384 + y, 4, stride=32), :] = flows[8:12]

    turn(3, 7, 0, 64)
    arrive_high(0)
    arrive_high(-1)

    @pl.when(wrap)
    def _():
        broad.wait_recv()

    turn(7, 10, 0, 48)
    for k in range(16):
        one(1, 2 * k)
    for k in range(15):
        two(1, 2 * k)
    arrive_low(0)
    arrive_low(-1)
    arrive_head(0)
    arrive_head(-1)
    turn(0, 3, 0, 48)
    for k in range(16):
        one(0, 2 * k)
    for k in range(15):
        two(0, 2 * k)
    arrive_high(1)
    arrive_low(1)
    arrive_head(1)

    turn(7, 10, 48, 64)
    turn(0, 3, 48, 64)
    for h in (1, 0):
        for k in range(16, 18):
            one(h, 2 * k)
    for k in range(8):
        three(2 * k)
    for h in (1, 0):
        for k in range(15, 17):
            two(h, 2 * k)
    for k in range(8, 17):
        three(2 * k)
    for y in range(32):
        finish(y)
    out[128:256, :] = out[128:256, :] + xyp[:128]
    out[256:384, :] = xyp[128:256]
    out[384:512, :] = out[384:512, :] + xyp[256:]

    for ds, dr in SIDES:

        @pl.when(inside(ds, dr) & ~(head if ds == -1 else jnp.bool_(False)))
        def _():
            copies[ds, dr].wait_send()

    @pl.when(head)
    def _():
        broad.wait_send()


def local(image, first_kernel, first_bias, middle_kernel, middle_bias, last_kernel, last_bias):
    args = (
        image,
        first_kernel.reshape(3, 3, 32),
        first_bias.reshape(1, 32),
        middle_kernel,
        middle_bias.reshape(1, 32),
        last_kernel,
        last_bias.reshape(1, 3),
    )
    args = [pltpu.with_memory_space_constraint(a, pltpu.HBM) for a in args]
    shape = jax.ShapeDtypeStruct
    vmem = pl.BlockSpec(memory_space=pltpu.VMEM)
    flows = pl.pallas_call(
        kernel,
        out_shape=shape((512, 128), F32),
        in_specs=[pl.BlockSpec(memory_space=pltpu.HBM)] * 7,
        out_specs=vmem,
        scratch_shapes=[
            pltpu.VMEM((10, 64, 128), BF16),
            pltpu.VMEM((256, 48), BF16),
            pltpu.VMEM((2, 96, 480), BF16),
            pltpu.VMEM((48, 192), BF16),
            pltpu.VMEM((96, 128), F32),
            pltpu.VMEM((384, 128), F32),
            pltpu.VMEM((1024, 128), F32),
            pltpu.VMEM((256, 36 * 128), BF16),
            pltpu.VMEM((192, 34 * 128), BF16),
            pltpu.VMEM((48, 34 * 128), F32),
            pltpu.VMEM((3, 3, 32), BF16),
            pltpu.VMEM((1, 32), F32),
            pltpu.VMEM((3, 3, 32, 32), BF16),
            pltpu.VMEM((1, 32), F32),
            pltpu.VMEM((3, 3, 3, 32), BF16),
            pltpu.VMEM((1, 3), F32),
            pltpu.VMEM((512, 128), BF16),
            pltpu.VMEM((96, 480), BF16),
            pltpu.VMEM((48, 192), BF16),
            pltpu.VMEM((3, 64, 512), BF16),
            pltpu.VMEM((1152, 256), BF16),
            pltpu.VMEM((1152, 256), BF16),
            pltpu.VMEM((1152, 256), BF16),
            pltpu.VMEM((1088, 256), BF16),
            pltpu.SemaphoreType.DMA((7,)),
            pltpu.SemaphoreType.DMA((9,)),
            pltpu.SemaphoreType.DMA((9,)),
        ],
        compiler_params=pltpu.CompilerParams(collective_id=0, has_side_effects=True, vmem_limit_bytes=24 * 2**20),
    )(*args)
    return flows.reshape(4, 4, 32, 128)


def solution(mesh):
    placed = (P("slab", "row", None), P(), P(), P(), P(), P(), P())
    return jax.shard_map(
        local, mesh=mesh, in_specs=placed, out_specs=P(None, "slab", "row", None), check_vma=False
    )
```

```python
import jax
import jax.numpy as jnp
from jax import lax
from jax.experimental import pallas as pl
from jax.experimental.pallas import tpu as pltpu
from jax.sharding import PartitionSpec as P

MESH = pl.DeviceIdType.MESH
F32 = jnp.float32
BF16 = jnp.bfloat16

SIDES = [(ds, dr) for ds in (1, -1, 0) for dr in (-1, 0, 1) if ds or dr]
RUN = 32


def iota(shape, dim):
    return lax.broadcasted_iota(jnp.int32, shape, dim)


def spread(rows, lanes):
    return ((iota((rows, lanes), 1) & 31) == iota((rows, lanes), 0)).astype(BF16)


def dot(a, b):
    return jnp.dot(a, b, preferred_element_type=F32)


def span(step, own, low, high):
    return {0: own, 1: low, -1: high}[step]


def kernel(
    img, k1, b1, k2, b2, k3, b3,
    out,
    ext, w1z, w2z, w3z, b2c, xyp, imt, g1, g2, p3,
    k1v, b1v, k2v, b2v, k3v, b3v, w1x, w2x, w3x, imx, h1c, h1l, h1r, h2x,
    load_sem, send_sem, recv_sem,
):
    s = lax.axis_index("slab")
    r = lax.axis_index("row")
    slabs = lax.axis_size("slab")
    rows = lax.axis_size("row")
    place = lax.rem(s, RUN)
    wrap = (place == RUN - 1) & (s < slabs - 1)

    def inside(ds, dr):
        return (s + ds >= 0) & (s + ds < slabs) & (r + dr >= 0) & (r + dr < rows)

    corner = (s == 0) & (r == 0)

    def greets(ds, dr):
        to_corner = (s + ds == 0) & (r + dr == 0)
        return (wrap | (place == 0) | to_corner) if ds < 0 else to_corner

    def greeted_by(ds):
        return (wrap | ((place == RUN - 2) & (s < slabs - 2)) | corner) if ds > 0 else corner

    def aside(ds):
        return wrap if ds == 0 else jnp.bool_(False)

    barrier = pltpu.get_barrier_semaphore()
    greeted = jnp.int32(0)
    for ds, dr in SIDES:
        greeted += (inside(ds, dr) & ~greets(ds, dr) & ~aside(ds)).astype(jnp.int32)

    def greet(ds, dr):
        @pl.when(inside(ds, dr) & ~greeted_by(ds) & ~aside(ds))
        def _():
            pl.semaphore_signal(barrier, inc=1, device_id=(s + ds, r + dr), device_id_type=MESH)

    copies = {}
    for n, (ds, dr) in enumerate(SIDES):
        zs, zd = span(ds, ((0, 4), (3, 7)), ((1, 4), (0, 3)), ((0, 3), (7, 10)))
        ys, yd = span(dr, ((0, 32), (16, 48)), ((16, 32), (0, 16)), ((0, 16), (48, 64)))
        copies[ds, dr] = pltpu.make_async_remote_copy(
            src_ref=img.at[zs[0] : zs[1], ys[0] : ys[1]],
            dst_ref=ext.at[zd[0] : zd[1], yd[0] : yd[1]],
            send_sem=send_sem.at[n],
            recv_sem=recv_sem.at[n],
            device_id=(s + ds, r + dr),
            device_id_type=MESH,
        )

    broad = pltpu.make_async_remote_copy(
        src_ref=ext.at[3:6],
        dst_ref=ext.at[7:10],
        send_sem=send_sem.at[8],
        recv_sem=recv_sem.at[8],
        device_id=(s - 1, r),
        device_id_type=MESH,
    )
    head = (place == 0) & (s > 0)

    def meet_and_send():
        @pl.when(greeted > 0)
        def _():
            pl.semaphore_wait(barrier, greeted)

        for ds, dr in SIDES:

            @pl.when(inside(ds, dr) & ~greets(ds, dr) & ~aside(ds))
            def _():
                copies[ds, dr].start()

    def arrive(ds, dr):
        @pl.when(inside(ds, dr))
        def _():
            copies[-ds, -dr].wait_recv()

        @pl.when(inside(ds, dr) & greets(ds, dr))
        def _():
            copies[ds, dr].start()

    def arrive_head(dr):
        @pl.when(head & inside(-1, dr))
        def _():
            copies[1, -dr].wait_recv()
            if dr == 0:
                broad.start()

    greet(0, 1)
    greet(0, -1)

    @pl.when(wrap | corner)
    def _():
        meet_and_send()

    for ds in (1, -1):
        for dr in (0, 1, -1):
            greet(ds, dr)

    loads = [
        pltpu.make_async_copy(a, b, load_sem.at[n])
        for n, (a, b) in enumerate(
            [(img, ext.at[3:7, 16:48]), (k1, k1v), (b1, b1v), (k2, k2v), (b2, b2v), (k3, k3v), (b3, b3v)]
        )
    ]
    for load in loads:
        load.start()

    for ds, dr in SIDES:
        z0, z1 = {-1: (0, 3), 0: (3, 7), 1: (7, 10)}[ds]
        y0, y1 = {-1: (0, 16), 0: (16, 48), 1: (48, 64)}[dr]

        @pl.when(~inside(ds, dr) & ~(wrap if ds == 1 else jnp.bool_(False)))
        def _():
            ext[z0:z1, y0:y1, :] = jnp.zeros((z1 - z0, y1 - y0, 128), BF16)

    for z in range(10, 16):
        imt[pl.ds(z, 64, stride=16), :] = jnp.ones((64, 128), F32)
    for z in range(10):
        imt[pl.ds(z, 64, stride=16), :] = jnp.zeros((64, 128), F32)
    for load in loads:
        load.wait()

    bias = b1v[...]
    high = bias.astype(BF16).astype(F32)
    mid = (bias - high).astype(BF16).astype(F32)
    low = bias - high - mid
    pieces = [k1v[a].astype(F32)[b : b + 1] for a in range(3) for b in range(3)] + [high, mid, low]
    row = iota((16, 32), 0)
    kk = jnp.zeros((16, 32), F32)
    for n, piece in enumerate(pieces):
        kk = jnp.where(row == n, jnp.broadcast_to(piece, (16, 32)), kk)
    kt = dot(kk.astype(BF16), spread(32, 512))

    def taps(height, lanes, b, first):
        out = jnp.zeros((height, lanes), F32)
        gap = iota((height, lanes), 0) - (iota((height, lanes), 1) >> 5) - first
        for a in range(3):
            n = 3 * a + b
            out = jnp.where(gap == a, jnp.broadcast_to(kt[n : n + 1, :lanes], (height, lanes)), out)
        return out

    def biases(out, first):
        height, lanes = out.shape
        at = iota((height, lanes), 0) - first
        for m in range(3):
            out = jnp.where(at == m, jnp.broadcast_to(kt[9 + m : 10 + m, :lanes], (height, lanes)), out)
        return out

    tall = jnp.concatenate(
        [taps(32, 512, b, 13) for b in range(3)] + [biases(jnp.zeros((32, 512), F32), 0)], axis=0
    )
    w1x[...] = tall.T.astype(BF16)
    flat = jnp.concatenate(
        [taps(16, 256, 0, 0), biases(taps(16, 256, 1, 0), 10), taps(16, 256, 2, 0), jnp.zeros((80, 256), F32)], axis=0
    )
    w1z[...] = flat.T[:, :48].astype(BF16)

    lane = iota((32, 480), 1)
    wide = sum(
        dot(
            k2v[:, b].reshape(96, 32),
            ((lane >= 160 * b) & (lane < 160 * b + 160) & ((lane & 31) == iota((32, 480), 0))).astype(BF16),
        )
        for b in range(3)
    )
    part = (lane - jnp.where(lane >= 320, 320, jnp.where(lane >= 160, 160, 0))) >> 5

    def in_two(skip):
        z = s * 4 - 2 + skip + part
        return (z >= 0) & (z < 4 * slabs)

    for o in range(3):
        block = jnp.zeros((32, 480), F32)
        for a in range(3):
            block = jnp.where(part == o + a, wide[a * 32 : a * 32 + 32], block)
        w2x[o * 32 : o * 32 + 32, :] = block.astype(BF16)
        for h, skip in ((0, 0), (1, 3)):
            w2z[h, o * 32 : o * 32 + 32, :] = jnp.where(in_two(skip), block, 0.0).astype(BF16)
    column = jnp.sum(
        jnp.where(iota((32, 32), 0) == iota((32, 32), 1), jnp.broadcast_to(b2v[...], (32, 32)), 0.0), axis=1, keepdims=True
    )
    for o in range(3):
        b2c[o * 32 : o * 32 + 32, :] = jnp.broadcast_to(column, (32, 128))

    group = iota((48, 32), 0) >> 2
    lasts = []
    for a in range(3):
        last = jnp.zeros((48, 32), F32)
        for b in range(3):
            line = k3v[a, b].astype(F32)
            for f in range(3):
                last = jnp.where(group == 4 * b + f, jnp.broadcast_to(line[f : f + 1], (48, 32)), last)
        lasts.append(last)
    wide3 = dot(jnp.concatenate(lasts, axis=0).astype(BF16), spread(32, 192))
    part3 = (iota((48, 192), 1) >> 5) - (iota((48, 192), 0) & 3)
    last = jnp.zeros((48, 192), F32)
    for a in range(3):
        last = jnp.where(part3 == a, wide3[48 * a : 48 * a + 48], last)
    z_of = s * 4 + (iota((48, 192), 1) >> 5)
    w3x[...] = last.astype(BF16)
    w3z[...] = jnp.where((z_of >= 1) & (z_of < 4 * slabs + 1), last, 0.0).astype(BF16)

    kind = iota((16, 128), 0) >> 2
    flow = [jnp.broadcast_to(b3v[0:1, f : f + 1], (16, 128)) for f in range(3)]
    bias_yz = jnp.where(kind == 0, flow[0], 0.0)
    scale_yz = jnp.where(kind == 0, 1.0, 0.5)
    bias_xy = jnp.where(kind == 0, 0.5 * (flow[0] + flow[1]), jnp.where(kind == 1, flow[1], flow[2]))
    scale_xy = jnp.where(kind == 1, 1.0, 0.5)

    @pl.when(~wrap & ~corner)
    def _():
        meet_and_send()

    @pl.when(wrap)
    def _():
        arrive(-1, 0)
        for dr in (1, -1):

            @pl.when(inside(0, dr))
            def _():
                copies[0, dr].start()

        arrive(-1, 1)
        arrive(-1, -1)

    arrive(0, -1)

    bias_two = jnp.concatenate([b2c[...]] * 2, axis=1)

    def turn(z0, z1, y0, y1):
        for z in range(z0, z1):
            imt[pl.ds(16 * y0 + z, y1 - y0, stride=16), :] = ext[z, y0:y1, :].astype(F32)

    def arrive_high(dr):
        @pl.when(~wrap)
        def _():
            arrive(1, dr)

    def arrive_low(dr):
        @pl.when(~wrap & ~head)
        def _():
            arrive(-1, dr)

    top = jnp.where(r == 0, 0.0, 1.0)
    bottom = jnp.where(r == rows - 1, 0.0, 1.0)

    part_one = ((0, 96), (96, 256))

    def one(h, j):
        lo, hi = part_one[h]
        rhs = jnp.concatenate([imt[(j + i + 13) * 16 : (j + i + 16) * 16, :].astype(BF16) for i in range(2)], axis=1)
        hidden = jnp.maximum(dot(w1z[lo:hi], rhs), 0.0)
        if j == 0:
            hidden = hidden * top
        if j == 34:
            hidden = hidden * bottom
        g1[lo:hi, j * 128 : j * 128 + 256] = hidden.astype(BF16)

    def two(h, j):
        at = 96 * h
        rhs = jnp.concatenate([g1[at : at + 160, (j + b) * 128 : (j + b) * 128 + 256] for b in range(3)], axis=0)
        hidden = jnp.maximum(dot(w2z[h], rhs) + bias_two, 0.0)
        if j == 0:
            hidden = jnp.concatenate([hidden[:, :128] * top, hidden[:, 128:]], axis=1)
        if j == 32:
            hidden = jnp.concatenate([hidden[:, :128], hidden[:, 128:] * bottom], axis=1)
        g2[at : at + 96, j * 128 : j * 128 + 256] = hidden.astype(BF16)

    def three(j):
        p3[:, j * 128 : j * 128 + 256] = dot(w3z[...], g2[:, j * 128 : j * 128 + 256])

    def finish(y):
        total = sum(p3[16 * b : 16 * b + 16, (y + b) * 128 : (y + b) * 128 + 128] for b in range(3))
        flows = total * scale_yz + bias_yz
        out[pl.ds(y, 8, stride=32), :] = flows[:8]
        out[pl.ds(384 + y, 4, stride=32), :] = flows[8:12]

    def shifted(values, by):
        edge = iota((values.shape[0], 128), 1) == (0 if by > 0 else 127)
        halves = [jnp.where(edge, 0.0, pltpu.roll(values[:, h : h + 128], by % 128, 1)) for h in (0, 128)]
        return jnp.concatenate(halves, axis=1)


    def pair(t, carry):
        cols = pl.ds(pl.multiple_of(t * 256, 256), 256)
        for j, height in ((0, 512), (1, 512), (2, 128)):
            window = [imx[b, 16 * j : 16 * j + 32, cols] for b in range(3)]
            rhs = jnp.concatenate(window + [jnp.ones((32, 256), BF16)], axis=0)
            hidden = jnp.maximum(dot(w1x[:height], rhs), 0.0)
            h1c[512 * j : 512 * j + height] = hidden.astype(BF16)
            h1l[512 * j : 512 * j + height] = shifted(hidden, 1).astype(BF16)
            h1r[512 * j : 512 * j + height] = shifted(hidden, -1).astype(BF16)

        for ref in (h1c, h1l, h1r):

            @pl.when(r == 0)
            def _():
                ref[:64] = jnp.zeros((64, 256), BF16)

            @pl.when(r == rows - 1)
            def _():
                ref[1088:] = jnp.zeros((64, 256), BF16)

        for start in (0, 3, 6, 9, 12, 15, 18, 21, 24, 27, 30, 31):
            at = start * 32
            rhs = jnp.concatenate([ref[at : at + 160] for ref in (h1l, h1c, h1r)], axis=0)
            h2x[at : at + 96] = jnp.maximum(dot(w2x[...], rhs) + bias_two, 0.0).astype(BF16)

        @pl.when(r == 0)
        def _():
            h2x[:32] = jnp.zeros((32, 256), BF16)

        @pl.when(r == rows - 1)
        def _():
            h2x[1056:] = jnp.zeros((32, 256), BF16)

        for k in range(8):
            terms = dot(w3x[...], h2x[128 * k : 128 * k + 192])
            total = shifted(terms[:16], 1) + terms[16:32] + shifted(terms[32:], -1)
            for h in range(2):
                flows = total[:, 128 * h : 128 * h + 128] * scale_xy + bias_xy
                for f in range(3):
                    xyp[pl.ds((4 * f + 2 * t + h) * 32 + 4 * k, 4), :] = flows[4 * f : 4 * f + 4]
        return carry

    def along_x():
        arrive(0, 1)
        lane = iota((64, 128), 1)
        for z in range(4):
            plane = ext[3 + z].astype(F32)
            at = pl.ds(z * 128, 128)
            imx[0, :, at] = jnp.where(lane == 0, 0.0, pltpu.roll(plane, 1, 1)).astype(BF16)
            imx[1, :, at] = plane.astype(BF16)
            imx[2, :, at] = jnp.where(lane == 127, 0.0, pltpu.roll(plane, 127, 1)).astype(BF16)

        lax.fori_loop(0, 2, pair, 0)

    def high_half():
        arrive_high(0)
        arrive_high(-1)

        @pl.when(wrap)
        def _():
            broad.wait_recv()

        turn(7, 10, 0, 48)
        for k in range(16):
            one(1, 2 * k)
        for k in range(15):
            two(1, 2 * k)

    turn(3, 7, 0, 48)
    ahead = (r == 1) & (s > 0) & (place != RUN - 2)

    def either(t, carry):
        @pl.when((t == 0) ^ ahead)
        def _():
            along_x()

        @pl.when((t == 1) ^ ahead)
        def _():
            high_half()

        return carry

    lax.fori_loop(0, 2, either, 0)

    arrive_low(0)
    arrive_low(-1)
    arrive_head(0)
    arrive_head(-1)
    turn(0, 3, 0, 48)
    for k in range(16):
        one(0, 2 * k)
    for k in range(15):
        two(0, 2 * k)
    for k in range(15):
        three(2 * k)
    arrive_high(1)
    arrive_low(1)
    arrive_head(1)

    turn(0, 10, 48, 64)
    for h in (1, 0):
        for k in range(16, 18):
            one(h, 2 * k)
    for y in range(14):
        finish(y)
    for h in (1, 0):
        for k in range(15, 17):
            two(h, 2 * k)
    for y in range(14, 28):
        finish(y)
    for k in range(15, 17):
        three(2 * k)
    out[256:384, :] = xyp[128:256]
    for y in range(28, 32):
        finish(y)
    out[128:256, :] = out[128:256, :] + xyp[:128]
    out[384:512, :] = out[384:512, :] + xyp[256:]

    for ds, dr in SIDES:

        @pl.when(inside(ds, dr) & ~(head if ds == -1 else jnp.bool_(False)))
        def _():
            copies[ds, dr].wait_send()

    @pl.when(head)
    def _():
        broad.wait_send()


def local(image, first_kernel, first_bias, middle_kernel, middle_bias, last_kernel, last_bias):
    args = (
        image,
        first_kernel.reshape(3, 3, 32),
        first_bias.reshape(1, 32),
        middle_kernel,
        middle_bias.reshape(1, 32),
        last_kernel,
        last_bias.reshape(1, 3),
    )
    args = [pltpu.with_memory_space_constraint(a, pltpu.HBM) for a in args]
    shape = jax.ShapeDtypeStruct
    vmem = pl.BlockSpec(memory_space=pltpu.VMEM)
    flows = pl.pallas_call(
        kernel,
        out_shape=shape((512, 128), F32),
        in_specs=[pl.BlockSpec(memory_space=pltpu.HBM)] * 7,
        out_specs=vmem,
        scratch_shapes=[
            pltpu.VMEM((10, 64, 128), BF16),
            pltpu.VMEM((256, 48), BF16),
            pltpu.VMEM((2, 96, 480), BF16),
            pltpu.VMEM((48, 192), BF16),
            pltpu.VMEM((96, 128), F32),
            pltpu.VMEM((384, 128), F32),
            pltpu.VMEM((1024, 128), F32),
            pltpu.VMEM((256, 36 * 128), BF16),
            pltpu.VMEM((192, 34 * 128), BF16),
            pltpu.VMEM((48, 34 * 128), F32),
            pltpu.VMEM((3, 3, 32), BF16),
            pltpu.VMEM((1, 32), F32),
            pltpu.VMEM((3, 3, 32, 32), BF16),
            pltpu.VMEM((1, 32), F32),
            pltpu.VMEM((3, 3, 3, 32), BF16),
            pltpu.VMEM((1, 3), F32),
            pltpu.VMEM((512, 128), BF16),
            pltpu.VMEM((96, 480), BF16),
            pltpu.VMEM((48, 192), BF16),
            pltpu.VMEM((3, 64, 512), BF16),
            pltpu.VMEM((1152, 256), BF16),
            pltpu.VMEM((1152, 256), BF16),
            pltpu.VMEM((1152, 256), BF16),
            pltpu.VMEM((1088, 256), BF16),
            pltpu.SemaphoreType.DMA((7,)),
            pltpu.SemaphoreType.DMA((9,)),
            pltpu.SemaphoreType.DMA((9,)),
        ],
        compiler_params=pltpu.CompilerParams(collective_id=0, has_side_effects=True, vmem_limit_bytes=24 * 2**20),
    )(*args)
    return flows.reshape(4, 4, 32, 128)


def solution(mesh):
    placed = (P("slab", "row", None), P(), P(), P(), P(), P(), P())
    return jax.shard_map(
        local, mesh=mesh, in_specs=placed, out_specs=P(None, "slab", "row", None), check_vma=False
    )
```

```python
import jax
import jax.numpy as jnp
from jax import lax
from jax.experimental import pallas as pl
from jax.experimental.pallas import tpu as pltpu
from jax.sharding import PartitionSpec as P

MESH = pl.DeviceIdType.MESH
F32 = jnp.float32
BF16 = jnp.bfloat16

SIDES = [(ds, dr) for ds in (1, -1, 0) for dr in (-1, 0, 1) if ds or dr]
RUN = 32


def iota(shape, dim):
    return lax.broadcasted_iota(jnp.int32, shape, dim)


def spread(rows, lanes):
    return ((iota((rows, lanes), 1) & 31) == iota((rows, lanes), 0)).astype(BF16)


def dot(a, b):
    return jnp.dot(a, b, preferred_element_type=F32)


def span(step, own, low, high):
    return {0: own, 1: low, -1: high}[step]


def kernel(
    img, k1, b1, k2, b2, k3, b3,
    out,
    ext, w1z, w2z, w3z, b2c, imt, g1, g2, p3,
    k1v, b1v, k2v, b2v, k3v, b3v, w1x, w2x, w3x, imx, h1c, h1l, h1r, h2x,
    load_sem, send_sem, recv_sem, go_sem,
):
    s = lax.axis_index("slab")
    r = lax.axis_index("row")
    slabs = lax.axis_size("slab")
    rows = lax.axis_size("row")
    place = lax.rem(s, RUN)
    wrap = (place == RUN - 1) & (s < slabs - 1)

    def inside(ds, dr):
        return (s + ds >= 0) & (s + ds < slabs) & (r + dr >= 0) & (r + dr < rows)

    corner = (s == 0) & (r == 0)

    def greets(ds, dr):
        to_corner = (s + ds == 0) & (r + dr == 0)
        return (wrap | (place == 0) | to_corner) if ds < 0 else to_corner

    def greeted_by(ds):
        return (wrap | ((place == RUN - 2) & (s < slabs - 2)) | corner) if ds > 0 else corner

    def aside(ds):
        return wrap if ds == 0 else jnp.bool_(False)

    barrier = pltpu.get_barrier_semaphore()
    greeted = jnp.int32(0)
    for ds, dr in SIDES:
        greeted += (inside(ds, dr) & ~greets(ds, dr) & ~aside(ds)).astype(jnp.int32)

    def greet(ds, dr):
        @pl.when(inside(ds, dr) & ~greeted_by(ds) & ~aside(ds))
        def _():
            pl.semaphore_signal(barrier, inc=1, device_id=(s + ds, r + dr), device_id_type=MESH)

    copies = {}
    for n, (ds, dr) in enumerate(SIDES):
        zs, zd = span(ds, ((0, 4), (3, 7)), ((1, 4), (0, 3)), ((0, 3), (7, 10)))
        ys, yd = span(dr, ((0, 32), (16, 48)), ((16, 32), (0, 16)), ((0, 16), (48, 64)))
        copies[ds, dr] = pltpu.make_async_remote_copy(
            src_ref=img.at[zs[0] : zs[1], ys[0] : ys[1]],
            dst_ref=ext.at[zd[0] : zd[1], yd[0] : yd[1]],
            send_sem=send_sem.at[n],
            recv_sem=recv_sem.at[n],
            device_id=(s + ds, r + dr),
            device_id_type=MESH,
        )

    broad = pltpu.make_async_remote_copy(
        src_ref=ext.at[3:6],
        dst_ref=ext.at[7:10],
        send_sem=send_sem.at[8],
        recv_sem=recv_sem.at[8],
        device_id=(s - 1, r),
        device_id_type=MESH,
    )
    head = (place == 0) & (s > 0)

    def meet_and_send():
        @pl.when(greeted > 0)
        def _():
            pl.semaphore_wait(barrier, greeted)

        for ds, dr in SIDES:

            @pl.when(inside(ds, dr) & ~greets(ds, dr) & ~aside(ds))
            def _():
                copies[ds, dr].start()

    def arrive(ds, dr):
        @pl.when(inside(ds, dr))
        def _():
            copies[-ds, -dr].wait_recv()

        @pl.when(inside(ds, dr) & greets(ds, dr))
        def _():
            copies[ds, dr].start()

    def arrive_head(dr):
        @pl.when(head & inside(-1, dr))
        def _():
            copies[1, -dr].wait_recv()

    greet(0, 1)
    greet(0, -1)

    @pl.when(wrap | corner)
    def _():
        meet_and_send()

    @pl.when(wrap)
    def _():
        pl.semaphore_signal(go_sem, inc=1, device_id=(s + 1, r), device_id_type=MESH)

    for ds in (1, -1):
        for dr in (0, 1, -1):
            greet(ds, dr)

    loads = [
        pltpu.make_async_copy(a, b, load_sem.at[n])
        for n, (a, b) in enumerate(
            [(img, ext.at[3:7, 16:48]), (k1, k1v), (b1, b1v), (k2, k2v), (b2, b2v), (k3, k3v), (b3, b3v)]
        )
    ]
    for load in loads:
        load.start()

    for ds, dr in SIDES:
        z0, z1 = {-1: (0, 3), 0: (3, 7), 1: (7, 10)}[ds]
        y0, y1 = {-1: (0, 16), 0: (16, 48), 1: (48, 64)}[dr]

        @pl.when(~inside(ds, dr) & ~(wrap if ds == 1 else jnp.bool_(False)))
        def _():
            ext[z0:z1, y0:y1, :] = jnp.zeros((z1 - z0, y1 - y0, 128), BF16)

    for z in range(10, 16):
        imt[pl.ds(z, 64, stride=16), :] = jnp.ones((64, 128), F32)
    for z in range(10):
        imt[pl.ds(z, 64, stride=16), :] = jnp.zeros((64, 128), F32)
    for load in loads:
        load.wait()

    bias = b1v[...]
    high = bias.astype(BF16).astype(F32)
    mid = (bias - high).astype(BF16).astype(F32)
    low = bias - high - mid
    pieces = [k1v[a].astype(F32)[b : b + 1] for a in range(3) for b in range(3)] + [high, mid, low]
    row = iota((16, 32), 0)
    kk = jnp.zeros((16, 32), F32)
    for n, piece in enumerate(pieces):
        kk = jnp.where(row == n, jnp.broadcast_to(piece, (16, 32)), kk)
    kt = dot(kk.astype(BF16), spread(32, 512))

    def taps(height, lanes, b, first):
        out = jnp.zeros((height, lanes), F32)
        gap = iota((height, lanes), 0) - (iota((height, lanes), 1) >> 5) - first
        for a in range(3):
            n = 3 * a + b
            out = jnp.where(gap == a, jnp.broadcast_to(kt[n : n + 1, :lanes], (height, lanes)), out)
        return out

    def biases(out, first):
        height, lanes = out.shape
        at = iota((height, lanes), 0) - first
        for m in range(3):
            out = jnp.where(at == m, jnp.broadcast_to(kt[9 + m : 10 + m, :lanes], (height, lanes)), out)
        return out

    tall = jnp.concatenate(
        [taps(32, 512, b, 13) for b in range(3)] + [biases(jnp.zeros((32, 512), F32), 0)], axis=0
    )
    w1x[...] = tall.T.astype(BF16)
    flat = jnp.concatenate(
        [taps(16, 256, 0, 0), biases(taps(16, 256, 1, 0), 10), taps(16, 256, 2, 0), jnp.zeros((80, 256), F32)], axis=0
    )
    w1z[...] = flat.T[:, :48].astype(BF16)

    lane = iota((32, 480), 1)
    wide = sum(
        dot(
            k2v[:, b].reshape(96, 32),
            ((lane >= 160 * b) & (lane < 160 * b + 160) & ((lane & 31) == iota((32, 480), 0))).astype(BF16),
        )
        for b in range(3)
    )
    part = (lane - jnp.where(lane >= 320, 320, jnp.where(lane >= 160, 160, 0))) >> 5

    def in_two(skip):
        z = s * 4 - 2 + skip + part
        return (z >= 0) & (z < 4 * slabs)

    for o in range(3):
        block = jnp.zeros((32, 480), F32)
        for a in range(3):
            block = jnp.where(part == o + a, wide[a * 32 : a * 32 + 32], block)
        w2x[o * 32 : o * 32 + 32, :] = block.astype(BF16)
        for h, skip in ((0, 0), (1, 3)):
            w2z[h, o * 32 : o * 32 + 32, :] = jnp.where(in_two(skip), block, 0.0).astype(BF16)
    column = jnp.sum(
        jnp.where(iota((32, 32), 0) == iota((32, 32), 1), jnp.broadcast_to(b2v[...], (32, 32)), 0.0), axis=1, keepdims=True
    )
    for o in range(3):
        b2c[o * 32 : o * 32 + 32, :] = jnp.broadcast_to(column, (32, 128))

    group = iota((48, 32), 0) >> 2
    lasts = []
    for a in range(3):
        last = jnp.zeros((48, 32), F32)
        for b in range(3):
            line = k3v[a, b].astype(F32)
            for f in range(3):
                last = jnp.where(group == 4 * b + f, jnp.broadcast_to(line[f : f + 1], (48, 32)), last)
        lasts.append(last)
    wide3 = dot(jnp.concatenate(lasts, axis=0).astype(BF16), spread(32, 192))
    part3 = (iota((48, 192), 1) >> 5) - (iota((48, 192), 0) & 3)
    last = jnp.zeros((48, 192), F32)
    for a in range(3):
        last = jnp.where(part3 == a, wide3[48 * a : 48 * a + 48], last)
    z_of = s * 4 + (iota((48, 192), 1) >> 5)
    w3x[...] = last.astype(BF16)
    w3z[...] = jnp.where((z_of >= 1) & (z_of < 4 * slabs + 1), last, 0.0).astype(BF16)

    kind = iota((16, 128), 0) >> 2
    flow = [jnp.broadcast_to(b3v[0:1, f : f + 1], (16, 128)) for f in range(3)]
    out[0:128, :] = jnp.broadcast_to(b3v[0:1, 0:1], (128, 128))
    scale_yz = jnp.where(kind == 0, 1.0, 0.5)
    bias_xy = jnp.where(kind == 0, 0.5 * (flow[0] + flow[1]), jnp.where(kind == 1, flow[1], flow[2]))
    scale_xy = jnp.where(kind == 1, 1.0, 0.5)

    @pl.when(~wrap & ~corner)
    def _():
        meet_and_send()

    @pl.when(wrap)
    def _():
        arrive(-1, 0)
        for dr in (1, -1):

            @pl.when(inside(0, dr))
            def _():
                copies[0, dr].start()

        arrive(-1, 1)
        arrive(-1, -1)

    arrive(0, -1)

    bias_two = jnp.concatenate([b2c[...]] * 2, axis=1)

    def turn(z0, z1, y0, y1):
        for z in range(z0, z1):
            imt[pl.ds(16 * y0 + z, y1 - y0, stride=16), :] = ext[z, y0:y1, :].astype(F32)

    def arrive_high(dr):
        @pl.when(~wrap)
        def _():
            arrive(1, dr)

    def arrive_low(dr):
        @pl.when(~wrap & ~head)
        def _():
            arrive(-1, dr)

    top = jnp.where(r == 0, 0.0, 1.0)
    bottom = jnp.where(r == rows - 1, 0.0, 1.0)

    part_one = ((0, 96), (96, 256))

    def one(h, j):
        lo, hi = part_one[h]
        rhs = jnp.concatenate([imt[(j + i + 13) * 16 : (j + i + 16) * 16, :].astype(BF16) for i in range(2)], axis=1)
        hidden = jnp.maximum(dot(w1z[lo:hi], rhs), 0.0)
        if j == 0:
            hidden = hidden * top
        if j == 34:
            hidden = hidden * bottom
        g1[lo:hi, j * 128 : j * 128 + 256] = hidden.astype(BF16)

    def two(h, j):
        at = 96 * h
        rhs = jnp.concatenate([g1[at : at + 160, (j + b) * 128 : (j + b) * 128 + 256] for b in range(3)], axis=0)
        hidden = jnp.maximum(dot(w2z[h], rhs) + bias_two, 0.0)
        if j == 0:
            hidden = jnp.concatenate([hidden[:, :128] * top, hidden[:, 128:]], axis=1)
        if j == 32:
            hidden = jnp.concatenate([hidden[:, :128], hidden[:, 128:] * bottom], axis=1)
        g2[at : at + 96, j * 128 : j * 128 + 256] = hidden.astype(BF16)

    def three(j):
        p3[:, j * 128 : j * 128 + 256] = dot(w3z[...], g2[:, j * 128 : j * 128 + 256])

    def finish(y):
        total = sum(p3[16 * b : 16 * b + 16, (y + b) * 128 : (y + b) * 128 + 128] for b in range(3))
        flows = total * scale_yz
        for lo, hi, at in ((0, 8, pl.ds(y, 8, stride=32)), (8, 12, pl.ds(384 + y, 4, stride=32))):
            out[at, :] = out[at, :] + flows[lo:hi]

    def shifted(values, by):
        edge = iota((values.shape[0], 128), 1) == (0 if by > 0 else 127)
        halves = [jnp.where(edge, 0.0, pltpu.roll(values[:, h : h + 128], by % 128, 1)) for h in (0, 128)]
        return jnp.concatenate(halves, axis=1)


    def pair(t, carry):
        cols = pl.ds(pl.multiple_of(t * 256, 256), 256)
        for j, height in ((0, 512), (1, 512), (2, 128)):
            window = [imx[b, 16 * j : 16 * j + 32, cols] for b in range(3)]
            rhs = jnp.concatenate(window + [jnp.ones((32, 256), BF16)], axis=0)
            hidden = jnp.maximum(dot(w1x[:height], rhs), 0.0)
            h1c[512 * j : 512 * j + height] = hidden.astype(BF16)
            h1l[512 * j : 512 * j + height] = shifted(hidden, 1).astype(BF16)
            h1r[512 * j : 512 * j + height] = shifted(hidden, -1).astype(BF16)

        for ref in (h1c, h1l, h1r):

            @pl.when(r == 0)
            def _():
                ref[:64] = jnp.zeros((64, 256), BF16)

            @pl.when(r == rows - 1)
            def _():
                ref[1088:] = jnp.zeros((64, 256), BF16)

        for start in (0, 3, 6, 9, 12, 15, 18, 21, 24, 27, 30, 31):
            at = start * 32
            rhs = jnp.concatenate([ref[at : at + 160] for ref in (h1l, h1c, h1r)], axis=0)
            h2x[at : at + 96] = jnp.maximum(dot(w2x[...], rhs) + bias_two, 0.0).astype(BF16)

        @pl.when(r == 0)
        def _():
            h2x[:32] = jnp.zeros((32, 256), BF16)

        @pl.when(r == rows - 1)
        def _():
            h2x[1056:] = jnp.zeros((32, 256), BF16)

        for k in range(8):
            terms = dot(w3x[...], h2x[128 * k : 128 * k + 192])
            total = shifted(terms[:16], 1) + terms[16:32] + shifted(terms[32:], -1)
            for h in range(2):
                flows = total[:, 128 * h : 128 * h + 128] * scale_xy + bias_xy
                for f in range(3):
                    out[pl.ds((4 * f + 4 + 2 * t + h) * 32 + 4 * k, 4), :] = flows[4 * f : 4 * f + 4]
        return carry

    def along_x():
        arrive(0, 1)
        lane = iota((64, 128), 1)
        for z in range(4):
            plane = ext[3 + z].astype(F32)
            at = pl.ds(z * 128, 128)
            imx[0, :, at] = jnp.where(lane == 0, 0.0, pltpu.roll(plane, 1, 1)).astype(BF16)
            imx[1, :, at] = plane.astype(BF16)
            imx[2, :, at] = jnp.where(lane == 127, 0.0, pltpu.roll(plane, 127, 1)).astype(BF16)

        lax.fori_loop(0, 2, pair, 0)

    def high_half():
        arrive_high(0)
        arrive_high(-1)

        @pl.when(wrap)
        def _():
            broad.wait_recv()

        turn(7, 10, 0, 48)
        for k in range(16):
            one(1, 2 * k)
        for k in range(15):
            two(1, 2 * k)

    turn(3, 7, 0, 48)
    ahead = (r == 1) & (s > 0) & (place != RUN - 2)

    def either(t, carry):
        @pl.when((t == 0) ^ ahead)
        def _():
            along_x()

        @pl.when((t == 1) ^ ahead)
        def _():
            high_half()

        return carry

    lax.fori_loop(0, 2, either, 0)

    @pl.when(head)
    def _():
        pl.semaphore_wait(go_sem, 1)
        broad.start()

    arrive_high(1)
    turn(3, 10, 48, 64)
    for k in range(16, 18):
        one(1, 2 * k)
    for k in range(15, 17):
        two(1, 2 * k)
    arrive_low(0)
    arrive_low(-1)
    arrive_head(0)
    arrive_head(-1)
    turn(0, 3, 0, 48)
    for k in range(16):
        one(0, 2 * k)
    for k in range(15):
        two(0, 2 * k)
    for k in range(15):
        three(2 * k)
        if k >= 3:
            finish(2 * k - 6)
            finish(2 * k - 5)
    arrive_low(1)
    arrive_head(1)
    turn(0, 3, 48, 64)
    for k in range(16, 18):
        one(0, 2 * k)
    for k in range(15, 17):
        two(0, 2 * k)
    for y in range(24, 28):
        finish(y)
    for k in range(15, 17):
        three(2 * k)
    for y in range(28, 32):
        finish(y)

    for ds, dr in SIDES:

        @pl.when(inside(ds, dr) & ~(head if ds == -1 else jnp.bool_(False)))
        def _():
            copies[ds, dr].wait_send()

    @pl.when(head)
    def _():
        broad.wait_send()


def local(image, first_kernel, first_bias, middle_kernel, middle_bias, last_kernel, last_bias):
    args = (
        image,
        first_kernel.reshape(3, 3, 32),
        first_bias.reshape(1, 32),
        middle_kernel,
        middle_bias.reshape(1, 32),
        last_kernel,
        last_bias.reshape(1, 3),
    )
    args = [pltpu.with_memory_space_constraint(a, pltpu.HBM) for a in args]
    shape = jax.ShapeDtypeStruct
    vmem = pl.BlockSpec(memory_space=pltpu.VMEM)
    flows = pl.pallas_call(
        kernel,
        out_shape=shape((512, 128), F32),
        in_specs=[pl.BlockSpec(memory_space=pltpu.HBM)] * 7,
        out_specs=vmem,
        scratch_shapes=[
            pltpu.VMEM((10, 64, 128), BF16),
            pltpu.VMEM((256, 48), BF16),
            pltpu.VMEM((2, 96, 480), BF16),
            pltpu.VMEM((48, 192), BF16),
            pltpu.VMEM((96, 128), F32),
            pltpu.VMEM((1024, 128), F32),
            pltpu.VMEM((256, 36 * 128), BF16),
            pltpu.VMEM((192, 34 * 128), BF16),
            pltpu.VMEM((48, 34 * 128), F32),
            pltpu.VMEM((3, 3, 32), BF16),
            pltpu.VMEM((1, 32), F32),
            pltpu.VMEM((3, 3, 32, 32), BF16),
            pltpu.VMEM((1, 32), F32),
            pltpu.VMEM((3, 3, 3, 32), BF16),
            pltpu.VMEM((1, 3), F32),
            pltpu.VMEM((512, 128), BF16),
            pltpu.VMEM((96, 480), BF16),
            pltpu.VMEM((48, 192), BF16),
            pltpu.VMEM((3, 64, 512), BF16),
            pltpu.VMEM((1152, 256), BF16),
            pltpu.VMEM((1152, 256), BF16),
            pltpu.VMEM((1152, 256), BF16),
            pltpu.VMEM((1088, 256), BF16),
            pltpu.SemaphoreType.DMA((7,)),
            pltpu.SemaphoreType.DMA((9,)),
            pltpu.SemaphoreType.DMA((9,)),
            pltpu.SemaphoreType.REGULAR,
        ],
        compiler_params=pltpu.CompilerParams(collective_id=0, has_side_effects=True, vmem_limit_bytes=24 * 2**20),
    )(*args)
    return flows.reshape(4, 4, 32, 128)


def solution(mesh):
    placed = (P("slab", "row", None), P(), P(), P(), P(), P(), P())
    return jax.shard_map(
        local, mesh=mesh, in_specs=placed, out_specs=P(None, "slab", "row", None), check_vma=False
    )
```

```python
import jax
import jax.numpy as jnp
from jax import lax
from jax.experimental import pallas as pl
from jax.experimental.pallas import tpu as pltpu
from jax.sharding import PartitionSpec as P

MESH = pl.DeviceIdType.MESH
F32 = jnp.float32
BF16 = jnp.bfloat16

SIDES = [(ds, dr) for ds in (1, -1, 0) for dr in (-1, 0, 1) if ds or dr]
RUN = 32


def iota(shape, dim):
    return lax.broadcasted_iota(jnp.int32, shape, dim)


def spread(rows, lanes):
    return ((iota((rows, lanes), 1) & 31) == iota((rows, lanes), 0)).astype(BF16)


def dot(a, b):
    return jnp.dot(a, b, preferred_element_type=F32)


def span(step, own, low, high):
    return {0: own, 1: low, -1: high}[step]


def kernel(
    img, k1, b1, k2, b2, k3, b3,
    out,
    ext, w1z, w2z, w3z, b2c, imt, g1, g2, p3,
    k1v, b1v, k2v, b2v, k3v, b3v, w1x, w2x, w3x, imx, h1c, h1l, h1r, h2x,
    load_sem, send_sem, recv_sem, go_sem,
):
    s = lax.axis_index("slab")
    r = lax.axis_index("row")
    slabs = lax.axis_size("slab")
    rows = lax.axis_size("row")
    place = lax.rem(s, RUN)
    wrap = (place == RUN - 1) & (s < slabs - 1)

    def inside(ds, dr):
        return (s + ds >= 0) & (s + ds < slabs) & (r + dr >= 0) & (r + dr < rows)

    corner = (s == 0) & (r == 0)

    def greets(ds, dr):
        to_corner = (s + ds == 0) & (r + dr == 0)
        return (wrap | (place == 0) | to_corner) if ds < 0 else to_corner

    def greeted_by(ds):
        return (wrap | ((place == RUN - 2) & (s < slabs - 2)) | corner) if ds > 0 else corner

    def aside(ds):
        return wrap if ds == 0 else jnp.bool_(False)

    barrier = pltpu.get_barrier_semaphore()
    greeted = jnp.int32(0)
    for ds, dr in SIDES:
        greeted += (inside(ds, dr) & ~greets(ds, dr) & ~aside(ds)).astype(jnp.int32)

    def greet(ds, dr):
        @pl.when(inside(ds, dr) & ~greeted_by(ds) & ~aside(ds))
        def _():
            pl.semaphore_signal(barrier, inc=1, device_id=(s + ds, r + dr), device_id_type=MESH)

    copies = {}
    for n, (ds, dr) in enumerate(SIDES):
        zs, zd = span(ds, ((0, 4), (3, 7)), ((1, 4), (0, 3)), ((0, 3), (7, 10)))
        ys, yd = span(dr, ((0, 32), (16, 48)), ((16, 32), (0, 16)), ((0, 16), (48, 64)))
        copies[ds, dr] = pltpu.make_async_remote_copy(
            src_ref=img.at[zs[0] : zs[1], ys[0] : ys[1]],
            dst_ref=ext.at[zd[0] : zd[1], yd[0] : yd[1]],
            send_sem=send_sem.at[n],
            recv_sem=recv_sem.at[n],
            device_id=(s + ds, r + dr),
            device_id_type=MESH,
        )

    broad = pltpu.make_async_remote_copy(
        src_ref=ext.at[3:6],
        dst_ref=ext.at[7:10],
        send_sem=send_sem.at[8],
        recv_sem=recv_sem.at[8],
        device_id=(s - 1, r),
        device_id_type=MESH,
    )
    head = (place == 0) & (s > 0)

    def meet_and_send():
        @pl.when(greeted > 0)
        def _():
            pl.semaphore_wait(barrier, greeted)

        for ds, dr in SIDES:

            @pl.when(inside(ds, dr) & ~greets(ds, dr) & ~aside(ds))
            def _():
                copies[ds, dr].start()

    def arrive(ds, dr):
        @pl.when(inside(ds, dr))
        def _():
            copies[-ds, -dr].wait_recv()

        @pl.when(inside(ds, dr) & greets(ds, dr))
        def _():
            copies[ds, dr].start()

    def arrive_head(dr):
        @pl.when(head & inside(-1, dr))
        def _():
            copies[1, -dr].wait_recv()

    greet(0, 1)
    greet(0, -1)

    @pl.when(wrap | corner)
    def _():
        meet_and_send()

    @pl.when(wrap)
    def _():
        pl.semaphore_signal(go_sem, inc=1, device_id=(s + 1, r), device_id_type=MESH)

    for ds in (1, -1):
        for dr in (0, 1, -1):
            greet(ds, dr)

    loads = [
        pltpu.make_async_copy(a, b, load_sem.at[n])
        for n, (a, b) in enumerate(
            [(img, ext.at[3:7, 16:48]), (k1, k1v), (b1, b1v), (k2, k2v), (b2, b2v), (k3, k3v), (b3, b3v)]
        )
    ]
    for load in loads:
        load.start()

    for ds, dr in SIDES:
        z0, z1 = {-1: (0, 3), 0: (3, 7), 1: (7, 10)}[ds]
        y0, y1 = {-1: (0, 16), 0: (16, 48), 1: (48, 64)}[dr]

        @pl.when(~inside(ds, dr) & ~(wrap if ds == 1 else jnp.bool_(False)))
        def _():
            ext[z0:z1, y0:y1, :] = jnp.zeros((z1 - z0, y1 - y0, 128), BF16)

    for z in range(10, 16):
        imt[pl.ds(z, 64, stride=16), :] = jnp.ones((64, 128), F32)
    for z in range(10):
        imt[pl.ds(z, 64, stride=16), :] = jnp.zeros((64, 128), F32)
    for load in loads:
        load.wait()

    bias = b1v[...]
    high = bias.astype(BF16).astype(F32)
    mid = (bias - high).astype(BF16).astype(F32)
    low = bias - high - mid
    pieces = [k1v[a].astype(F32)[b : b + 1] for a in range(3) for b in range(3)] + [high, mid, low]
    row = iota((16, 32), 0)
    kk = jnp.zeros((16, 32), F32)
    for n, piece in enumerate(pieces):
        kk = jnp.where(row == n, jnp.broadcast_to(piece, (16, 32)), kk)
    kt = dot(kk.astype(BF16), spread(32, 512))

    def taps(height, lanes, b, first):
        out = jnp.zeros((height, lanes), F32)
        gap = iota((height, lanes), 0) - (iota((height, lanes), 1) >> 5) - first
        for a in range(3):
            n = 3 * a + b
            out = jnp.where(gap == a, jnp.broadcast_to(kt[n : n + 1, :lanes], (height, lanes)), out)
        return out

    def biases(out, first):
        height, lanes = out.shape
        at = iota((height, lanes), 0) - first
        for m in range(3):
            out = jnp.where(at == m, jnp.broadcast_to(kt[9 + m : 10 + m, :lanes], (height, lanes)), out)
        return out

    tall = jnp.concatenate(
        [taps(32, 512, b, 13) for b in range(3)] + [biases(jnp.zeros((32, 512), F32), 0)], axis=0
    )
    w1x[...] = tall.T.astype(BF16)
    flat = jnp.concatenate(
        [taps(16, 256, 0, 0), biases(taps(16, 256, 1, 0), 10), taps(16, 256, 2, 0), jnp.zeros((80, 256), F32)], axis=0
    )
    w1z[...] = flat.T[:, :48].astype(BF16)

    lane = iota((32, 480), 1)
    wide = sum(
        dot(
            k2v[:, b].reshape(96, 32),
            ((lane >= 160 * b) & (lane < 160 * b + 160) & ((lane & 31) == iota((32, 480), 0))).astype(BF16),
        )
        for b in range(3)
    )
    part = (lane - jnp.where(lane >= 320, 320, jnp.where(lane >= 160, 160, 0))) >> 5

    def in_two(skip):
        z = s * 4 - 2 + skip + part
        return (z >= 0) & (z < 4 * slabs)

    for o in range(3):
        block = jnp.zeros((32, 480), F32)
        for a in range(3):
            block = jnp.where(part == o + a, wide[a * 32 : a * 32 + 32], block)
        w2x[o * 32 : o * 32 + 32, :] = block.astype(BF16)
        for h, skip in ((0, 0), (1, 3)):
            w2z[h, o * 32 : o * 32 + 32, :] = jnp.where(in_two(skip), block, 0.0).astype(BF16)
    column = jnp.sum(
        jnp.where(iota((32, 32), 0) == iota((32, 32), 1), jnp.broadcast_to(b2v[...], (32, 32)), 0.0), axis=1, keepdims=True
    )
    for o in range(3):
        b2c[o * 32 : o * 32 + 32, :] = jnp.broadcast_to(column, (32, 128))

    group = iota((48, 32), 0) >> 2
    lasts = []
    for a in range(3):
        last = jnp.zeros((48, 32), F32)
        for b in range(3):
            line = k3v[a, b].astype(F32)
            for f in range(3):
                last = jnp.where(group == 4 * b + f, jnp.broadcast_to(line[f : f + 1], (48, 32)), last)
        lasts.append(last)
    wide3 = dot(jnp.concatenate(lasts, axis=0).astype(BF16), spread(32, 192))
    part3 = (iota((48, 192), 1) >> 5) - (iota((48, 192), 0) & 3)
    last = jnp.zeros((48, 192), F32)
    for a in range(3):
        last = jnp.where(part3 == a, wide3[48 * a : 48 * a + 48], last)
    z_of = s * 4 + (iota((48, 192), 1) >> 5)
    w3x[...] = last.astype(BF16)
    in_three = (z_of >= 1) & (z_of < 4 * slabs + 1)
    w3z[0] = jnp.where(in_three, last, 0.0)[:, :96].astype(BF16)
    lane3 = (iota((48, 96), 1) >> 5) + 3
    upper = jnp.zeros((48, 96), F32)
    for a in range(3):
        upper = jnp.where(lane3 - (iota((48, 96), 0) & 3) == a, wide3[48 * a : 48 * a + 48, :96], upper)
    z_of = s * 4 + lane3
    w3z[1] = jnp.where((z_of >= 1) & (z_of < 4 * slabs + 1), upper, 0.0).astype(BF16)

    kind = iota((16, 128), 0) >> 2
    flow = [jnp.broadcast_to(b3v[0:1, f : f + 1], (16, 128)) for f in range(3)]
    out[0:128, :] = jnp.broadcast_to(b3v[0:1, 0:1], (128, 128))
    scale_yz = jnp.where(kind == 0, 1.0, 0.5)
    bias_xy = jnp.where(kind == 0, 0.5 * (flow[0] + flow[1]), jnp.where(kind == 1, flow[1], flow[2]))
    scale_xy = jnp.where(kind == 1, 1.0, 0.5)

    @pl.when(~wrap & ~corner)
    def _():
        meet_and_send()

    @pl.when(wrap)
    def _():
        arrive(-1, 0)
        for dr in (1, -1):

            @pl.when(inside(0, dr))
            def _():
                copies[0, dr].start()

        arrive(-1, 1)
        arrive(-1, -1)

    arrive(0, -1)

    bias_two = jnp.concatenate([b2c[...]] * 2, axis=1)

    def turn(z0, z1, y0, y1):
        for z in range(z0, z1):
            imt[pl.ds(16 * y0 + z, y1 - y0, stride=16), :] = ext[z, y0:y1, :].astype(F32)

    def arrive_high(dr):
        @pl.when(~wrap)
        def _():
            arrive(1, dr)

    def arrive_low(dr):
        @pl.when(~wrap & ~head)
        def _():
            arrive(-1, dr)

    top = jnp.where(r == 0, 0.0, 1.0)
    bottom = jnp.where(r == rows - 1, 0.0, 1.0)

    part_one = ((0, 96), (96, 256))

    def one(h, j):
        lo, hi = part_one[h]
        rhs = jnp.concatenate([imt[(j + i + 13) * 16 : (j + i + 16) * 16, :].astype(BF16) for i in range(2)], axis=1)
        hidden = jnp.maximum(dot(w1z[lo:hi], rhs), 0.0)
        if j == 0:
            hidden = hidden * top
        if j == 34:
            hidden = hidden * bottom
        g1[lo:hi, j * 128 : j * 128 + 256] = hidden.astype(BF16)

    def two(h, j):
        at = 96 * h
        rhs = jnp.concatenate([g1[at : at + 160, (j + b) * 128 : (j + b) * 128 + 256] for b in range(3)], axis=0)
        hidden = jnp.maximum(dot(w2z[h], rhs) + bias_two, 0.0)
        if j == 0:
            hidden = jnp.concatenate([hidden[:, :128] * top, hidden[:, 128:]], axis=1)
        if j == 32:
            hidden = jnp.concatenate([hidden[:, :128], hidden[:, 128:] * bottom], axis=1)
        g2[at : at + 96, j * 128 : j * 128 + 256] = hidden.astype(BF16)

    def three(h, j):
        at = slice(j * 128, j * 128 + 256)
        terms = dot(w3z[h], g2[96 * h : 96 * h + 96, at])
        p3[:, at] = terms if h else p3[:, at] + terms

    def finish(y):
        total = sum(p3[16 * b : 16 * b + 16, (y + b) * 128 : (y + b) * 128 + 128] for b in range(3))
        flows = total * scale_yz
        for lo, hi, at in ((0, 8, pl.ds(y, 8, stride=32)), (8, 12, pl.ds(384 + y, 4, stride=32))):
            out[at, :] = out[at, :] + flows[lo:hi]

    def shifted(values, by):
        edge = iota((values.shape[0], 128), 1) == (0 if by > 0 else 127)
        halves = [jnp.where(edge, 0.0, pltpu.roll(values[:, h : h + 128], by % 128, 1)) for h in (0, 128)]
        return jnp.concatenate(halves, axis=1)


    def pair(t, carry):
        cols = pl.ds(pl.multiple_of(t * 256, 256), 256)
        for j, height in ((0, 512), (1, 512), (2, 128)):
            window = [imx[b, 16 * j : 16 * j + 32, cols] for b in range(3)]
            rhs = jnp.concatenate(window + [jnp.ones((32, 256), BF16)], axis=0)
            hidden = jnp.maximum(dot(w1x[:height], rhs), 0.0)
            h1c[512 * j : 512 * j + height] = hidden.astype(BF16)
            h1l[512 * j : 512 * j + height] = shifted(hidden, 1).astype(BF16)
            h1r[512 * j : 512 * j + height] = shifted(hidden, -1).astype(BF16)

        for ref in (h1c, h1l, h1r):

            @pl.when(r == 0)
            def _():
                ref[:64] = jnp.zeros((64, 256), BF16)

            @pl.when(r == rows - 1)
            def _():
                ref[1088:] = jnp.zeros((64, 256), BF16)

        for start in (0, 3, 6, 9, 12, 15, 18, 21, 24, 27, 30, 31):
            at = start * 32
            rhs = jnp.concatenate([ref[at : at + 160] for ref in (h1l, h1c, h1r)], axis=0)
            h2x[at : at + 96] = jnp.maximum(dot(w2x[...], rhs) + bias_two, 0.0).astype(BF16)

        @pl.when(r == 0)
        def _():
            h2x[:32] = jnp.zeros((32, 256), BF16)

        @pl.when(r == rows - 1)
        def _():
            h2x[1056:] = jnp.zeros((32, 256), BF16)

        for k in range(8):
            terms = dot(w3x[...], h2x[128 * k : 128 * k + 192])
            total = shifted(terms[:16], 1) + terms[16:32] + shifted(terms[32:], -1)
            for h in range(2):
                flows = total[:, 128 * h : 128 * h + 128] * scale_xy + bias_xy
                for f in range(3):
                    out[pl.ds((4 * f + 4 + 2 * t + h) * 32 + 4 * k, 4), :] = flows[4 * f : 4 * f + 4]
        return carry

    def along_x():
        arrive(0, 1)
        lane = iota((64, 128), 1)
        for z in range(4):
            plane = ext[3 + z].astype(F32)
            at = pl.ds(z * 128, 128)
            imx[0, :, at] = jnp.where(lane == 0, 0.0, pltpu.roll(plane, 1, 1)).astype(BF16)
            imx[1, :, at] = plane.astype(BF16)
            imx[2, :, at] = jnp.where(lane == 127, 0.0, pltpu.roll(plane, 127, 1)).astype(BF16)

        lax.fori_loop(0, 2, pair, 0)

    def high_half():
        arrive_high(0)
        arrive_high(-1)

        @pl.when(wrap)
        def _():
            broad.wait_recv()

        turn(7, 10, 0, 48)
        for k in range(16):
            one(1, 2 * k)
        for k in range(15):
            two(1, 2 * k)
        for k in range(15):
            three(1, 2 * k)

    turn(3, 7, 0, 48)
    ahead = (r == 1) & (s > 0) & (place != RUN - 2)

    def either(t, carry):
        @pl.when((t == 0) ^ ahead)
        def _():
            along_x()

        @pl.when((t == 1) ^ ahead)
        def _():
            high_half()

        return carry

    lax.fori_loop(0, 2, either, 0)

    @pl.when(head)
    def _():
        pl.semaphore_wait(go_sem, 1)
        broad.start()

    arrive_high(1)
    turn(3, 10, 48, 64)
    for k in range(16, 18):
        one(1, 2 * k)
    for k in range(15, 17):
        two(1, 2 * k)
    for k in range(15, 17):
        three(1, 2 * k)
    arrive_low(0)
    arrive_low(-1)
    arrive_head(0)
    arrive_head(-1)
    turn(0, 3, 0, 48)
    for k in range(16):
        one(0, 2 * k)
    for k in range(15):
        two(0, 2 * k)
    for k in range(15):
        three(0, 2 * k)
        if k >= 3:
            finish(2 * k - 6)
            finish(2 * k - 5)
    arrive_low(1)
    arrive_head(1)
    turn(0, 3, 48, 64)
    for k in range(16, 18):
        one(0, 2 * k)
    for k in range(15, 17):
        two(0, 2 * k)
    for y in range(24, 28):
        finish(y)
    for k in range(15, 17):
        three(0, 2 * k)
    for y in range(28, 32):
        finish(y)

    for ds, dr in SIDES:

        @pl.when(inside(ds, dr) & ~(head if ds == -1 else jnp.bool_(False)))
        def _():
            copies[ds, dr].wait_send()

    @pl.when(head)
    def _():
        broad.wait_send()


def local(image, first_kernel, first_bias, middle_kernel, middle_bias, last_kernel, last_bias):
    args = (
        image,
        first_kernel.reshape(3, 3, 32),
        first_bias.reshape(1, 32),
        middle_kernel,
        middle_bias.reshape(1, 32),
        last_kernel,
        last_bias.reshape(1, 3),
    )
    args = [pltpu.with_memory_space_constraint(a, pltpu.HBM) for a in args]
    shape = jax.ShapeDtypeStruct
    vmem = pl.BlockSpec(memory_space=pltpu.VMEM)
    flows = pl.pallas_call(
        kernel,
        out_shape=shape((512, 128), F32),
        in_specs=[pl.BlockSpec(memory_space=pltpu.HBM)] * 7,
        out_specs=vmem,
        scratch_shapes=[
            pltpu.VMEM((10, 64, 128), BF16),
            pltpu.VMEM((256, 48), BF16),
            pltpu.VMEM((2, 96, 480), BF16),
            pltpu.VMEM((2, 48, 96), BF16),
            pltpu.VMEM((96, 128), F32),
            pltpu.VMEM((1024, 128), F32),
            pltpu.VMEM((256, 36 * 128), BF16),
            pltpu.VMEM((192, 34 * 128), BF16),
            pltpu.VMEM((48, 34 * 128), F32),
            pltpu.VMEM((3, 3, 32), BF16),
            pltpu.VMEM((1, 32), F32),
            pltpu.VMEM((3, 3, 32, 32), BF16),
            pltpu.VMEM((1, 32), F32),
            pltpu.VMEM((3, 3, 3, 32), BF16),
            pltpu.VMEM((1, 3), F32),
            pltpu.VMEM((512, 128), BF16),
            pltpu.VMEM((96, 480), BF16),
            pltpu.VMEM((48, 192), BF16),
            pltpu.VMEM((3, 64, 512), BF16),
            pltpu.VMEM((1152, 256), BF16),
            pltpu.VMEM((1152, 256), BF16),
            pltpu.VMEM((1152, 256), BF16),
            pltpu.VMEM((1088, 256), BF16),
            pltpu.SemaphoreType.DMA((7,)),
            pltpu.SemaphoreType.DMA((9,)),
            pltpu.SemaphoreType.DMA((9,)),
            pltpu.SemaphoreType.REGULAR,
        ],
        compiler_params=pltpu.CompilerParams(collective_id=0, has_side_effects=True, vmem_limit_bytes=24 * 2**20),
    )(*args)
    return flows.reshape(4, 4, 32, 128)


def solution(mesh):
    placed = (P("slab", "row", None), P(), P(), P(), P(), P(), P())
    return jax.shard_map(
        local, mesh=mesh, in_specs=placed, out_specs=P(None, "slab", "row", None), check_vma=False
    )
```
